512 devices in a mesh: dp: 2 (over core), ctx: 64 (over z, y), tensor: 4 (over x).
Axes of the slice: x: 4, y: 8, z: 8, core: 2. Of those that a mesh axis runs over, the one named last changes fastest.
Arguments:
- queries: bfloat16 [2, 8192, 4096], P('dp', 'ctx', 'tensor'), may hold values from -6 to 6
- keys: bfloat16 [2, 8192, 4096], P('dp', 'ctx', 'tensor'), may hold values from -6 to 6
- values: bfloat16 [2, 8192, 4096], P('dp', 'ctx', 'tensor'), may hold values from -6 to 6
- forget: float32 [2, 32, 8192], P('dp', 'tensor', 'ctx'), may hold values from 0 to 2
- gain: float32 [4096], P('tensor'), may hold values from 0.1 to 1.9
- grad_out: bfloat16 [2, 8192, 4096], P('dp', 'ctx', 'tensor'), may hold values from -8 to 8
Outputs:
- grad_queries: bfloat16 [2, 8192, 4096], P('dp', 'ctx', 'tensor')
- grad_keys: bfloat16 [2, 8192, 4096], P('dp', 'ctx', 'tensor')
- grad_values: bfloat16 [2, 8192, 4096], P('dp', 'ctx', 'tensor')
- grad_gain: float32 [4096], P('tensor')
The draws below stay inside these ranges and needn't reach their ends.
All inputs are finite; a program needn't handle non-finite values.
Results may differ from the reference program's by a relative error of at most 0.0062.
Values sent between devices are 32-bit elements; how exact they have to be, the bound alone decides.
A program may use at most 128 MiB of HBM per device.

```python
import math
import jax
import jax.numpy as jnp
from jax import lax

E = 128
TOK_DEV = 128
HEADS = 32
LENGTH = 8192
SEQS = 2
N_CTX = 64


def draw_forget(key, part):
    key = jax.random.fold_in(key, 7)
    pick_key, slow_key, fast_key, rough_key, spot_key, depth_key = jax.random.split(key, 6)
    slow_share = 0.5
    is_slow = jax.random.uniform(pick_key, (SEQS, HEADS, 1), dtype=jnp.float32) < slow_share
    slow_rate = jnp.exp(jax.random.uniform(slow_key, (SEQS, HEADS, 1), dtype=jnp.float32, minval=math.log(0.1), maxval=math.log(0.4))) / LENGTH
    fast_rate = jnp.exp(jax.random.uniform(fast_key, (SEQS, HEADS, 1), dtype=jnp.float32, minval=math.log(1.0 / 50.0), maxval=math.log(1.0 / 30.0)))
    rough = jnp.exp(jax.random.uniform(rough_key, (SEQS, HEADS, LENGTH), dtype=jnp.float32, minval=math.log(0.6), maxval=math.log(1.6)))
    spots = jax.random.randint(spot_key, (SEQS, 3, 1), 0, LENGTH)
    positions = jnp.arange(LENGTH)[None, None, :]
    hits = jnp.sum((positions == spots).astype(jnp.float32), axis=1)[:, None, :]
    depth = -jnp.log(1.0 - jax.random.uniform(depth_key, (SEQS, 1, LENGTH), dtype=jnp.float32, minval=0.2, maxval=0.4))
    rate = jnp.where(is_slow, slow_rate, fast_rate) * rough
    return (rate + hits * depth).astype(jnp.float32)


def draw_grad_out(key, part):
    key = jax.random.fold_in(key, 19)
    main_key = jax.random.fold_in(key, 0)
    positions = jnp.arange(LENGTH, dtype=jnp.float32)[None, :, None] / LENGTH
    noise = jax.random.normal(main_key, (SEQS, LENGTH, HEADS * E), dtype=jnp.float32)
    drawn = noise * (0.5 + positions)
    return jnp.clip(drawn, -8.0, 8.0).astype(jnp.bfloat16)


def block_scale(stream_key, shape, pieces, low, largest):
    loudness = 1.0
    for dim, parts in pieces:
        heights = jax.random.uniform(jax.random.fold_in(jax.random.fold_in(stream_key, 6), dim), (parts,), jnp.float32, low / len(pieces), largest / len(pieces))
        loudness = loudness * jnp.repeat(jnp.exp(heights), shape[dim] // parts).reshape((-1,) + (1,) * (len(shape) - 1 - dim))
    return loudness


def bell_draw(stream_key, shape, width, bound, cuts=(), kind=jnp.bfloat16):
    values = width * jax.random.normal(stream_key, shape, jnp.float32)
    if cuts:
        values = values * block_scale(stream_key, shape, cuts, -0.22, 0.18)
    return jnp.clip(values, -bound, bound).astype(kind)


def setup_inputs(seed: int = 0) -> dict:
    seeds = jax.random.split(jax.random.key(seed), 7)
    queries = bell_draw(seeds[0], (SEQS, LENGTH, HEADS * E), 1.0, 6.0, ((0, 2), (1, 64), (2, 4)))
    keys = bell_draw(seeds[1], (SEQS, LENGTH, HEADS * E), 1.0, 6.0, ((0, 2), (1, 64), (2, 4)))
    values = bell_draw(seeds[2], (SEQS, LENGTH, HEADS * E), 1.0, 6.0, ((0, 2), (1, 64), (2, 4)))
    forget = draw_forget(jax.random.fold_in(seeds[6], 71), 0)
    gain = jnp.clip(1.0 + 0.18 * jax.random.normal(seeds[4], (HEADS * E,), jnp.float32), 0.1, 1.9)
    grad_out = draw_grad_out(jax.random.fold_in(seeds[6], 71), 0)
    return {"queries": queries, "keys": keys, "values": values, "forget": forget, "gain": gain, "grad_out": grad_out}


EPSILON = 1e-05

def rounded(array_in):
    return lax.optimization_barrier(array_in.astype(jnp.bfloat16)).astype(jnp.float32)

def decay_parts(forget_now):
    cumulative = jnp.cumsum(forget_now, axis=1)
    spans_all = cumulative[:, :, None] - cumulative[:, None, :]
    positions = jnp.arange(forget_now.shape[1])
    lower_mask = (positions[:, None] >= positions[None, :])[None]
    weight = jnp.where(lower_mask, jnp.exp(-jnp.where(lower_mask, spans_all, 0.0)), 0.0)
    return (cumulative, weight)

def to_blocks(array_in):
    return array_in.reshape(N_CTX, TOK_DEV, HEADS, E).transpose(0, 2, 1, 3)

def from_blocks(array_in):
    return array_in.transpose(0, 2, 1, 3).reshape(LENGTH, HEADS * E)

def reference(queries, keys, values, forget, gain, grad_out):
    score_scale = E ** (-0.5)
    full_width = HEADS * E
    gain_sum = jnp.zeros((HEADS, E), jnp.float32)
    list_q, list_k, list_v = ([], [], [])
    zero_state = jnp.zeros((HEADS, E, E), jnp.float32)
    for sequence in range(SEQS):
        query_blocks = to_blocks(queries[sequence])
        key_blocks = to_blocks(keys[sequence])
        value_blocks = to_blocks(values[sequence])
        forget_blocks = forget[sequence].reshape(HEADS, N_CTX, TOK_DEV).transpose(1, 0, 2)
        grad_blocks = to_blocks(grad_out[sequence]).astype(jnp.float32)

        def forward(carried, inputs_now):
            query_now, key_now, value_now, forget_now = inputs_now
            cumulative, weight = decay_parts(forget_now)
            block_decay = cumulative[:, -1]
            query_f = query_now.astype(jnp.float32)
            key_f = key_now.astype(jnp.float32)
            value_f = value_now.astype(jnp.float32)
            weighted = rounded(jnp.einsum('hte,hse->hts', query_f, key_f) * score_scale * weight)
            attended = jnp.einsum('hts,hsf->htf', weighted, value_f) + score_scale * jnp.exp(-cumulative)[:, :, None] * jnp.einsum('hte,hef->htf', query_f, rounded(carried))
            key_scaled = rounded(key_f * jnp.exp(-(block_decay[:, None] - cumulative))[:, :, None])
            own_state = jnp.einsum('hse,hsf->hef', key_scaled, value_f)
            return (jnp.exp(-block_decay)[:, None, None] * carried + own_state, (attended, carried))
        _, (attended, earlier) = lax.scan(forward, zero_state, (query_blocks, key_blocks, value_blocks, forget_blocks))
        inverse_rms = lax.rsqrt(lax.optimization_barrier(jnp.sum(attended * attended, axis=(1, 3))) / full_width + EPSILON)
        normed = attended * inverse_rms[:, None, :, None]
        grad_normed = grad_blocks * gain.reshape(HEADS, E)[None, :, None, :]
        gain_sum = gain_sum + lax.optimization_barrier(jnp.sum(grad_blocks * normed, axis=(0, 2)))
        projected = lax.optimization_barrier(jnp.sum(grad_normed * normed, axis=(1, 3))) / full_width
        grad_attended = (inverse_rms[:, None, :, None] * (grad_normed - normed * projected[:, None, :, None])).astype(jnp.bfloat16)

        def backward(later_state, inputs_now):
            query_now, key_now, value_now, forget_now, carried, grad_now_b = inputs_now
            cumulative, weight = decay_parts(forget_now)
            block_decay = cumulative[:, -1]
            query_f = query_now.astype(jnp.float32)
            key_f = key_now.astype(jnp.float32)
            value_f = value_now.astype(jnp.float32)
            grad_now = grad_now_b.astype(jnp.float32)
            weighted = rounded(jnp.einsum('hte,hse->hts', query_f, key_f) * score_scale * weight)
            grad_weighted = rounded(jnp.einsum('htf,hsf->hts', grad_now, value_f) * score_scale * weight)
            query_decay = jnp.exp(-cumulative)[:, :, None]
            key_decay = jnp.exp(-(block_decay[:, None] - cumulative))[:, :, None]
            earlier_b = rounded(carried)
            later_b = rounded(later_state)
            grad_q = jnp.einsum('hts,hse->hte', grad_weighted, key_f) + score_scale * query_decay * jnp.einsum('htf,hef->hte', grad_now, earlier_b)
            grad_k = jnp.einsum('hts,hte->hse', grad_weighted, query_f) + score_scale * key_decay * jnp.einsum('hsf,hef->hse', value_f, later_b)
            grad_v = jnp.einsum('hts,htf->hsf', weighted, grad_now) + score_scale * key_decay * jnp.einsum('hse,hef->hsf', key_f, later_b)
            query_scaled = rounded(query_f * query_decay)
            own_back = jnp.einsum('hte,htf->hef', query_scaled, grad_now)
            next_state = jnp.exp(-block_decay)[:, None, None] * later_state + own_back
            return (next_state, (grad_q.astype(jnp.bfloat16), grad_k.astype(jnp.bfloat16), grad_v.astype(jnp.bfloat16)))
        _, (grad_q, grad_k, grad_v) = lax.scan(backward, zero_state, (query_blocks, key_blocks, value_blocks, forget_blocks, earlier, grad_attended), reverse=True)
        list_q.append(from_blocks(grad_q))
        list_k.append(from_blocks(grad_k))
        list_v.append(from_blocks(grad_v))
    return (jnp.stack(list_q), jnp.stack(list_k), jnp.stack(list_v), gain_sum.reshape(-1))
```

```python
import functools

import jax
import jax.numpy as jnp
from jax import lax
from jax.experimental import pallas as pl
from jax.experimental.pallas import tpu as pltpu
from jax.sharding import PartitionSpec as P

E = 128
EPSILON = 1e-05
MESH = pl.DeviceIdType.MESH
F32 = jnp.float32
BF16 = jnp.bfloat16

HEADS = 8
CTX = 64
RING = 8
TENSOR = 4
BATCHES = 2
GROUP = HEADS // BATCHES
OWNERS = CTX // GROUP


def matmul(a, b, contract_a, contract_b):
    return lax.dot_general(
        a, b, (((contract_a,), (contract_b,)), ((), ())), preferred_element_type=F32
    )


def kernel(
    q_ref, k_ref, v_ref, f_ref, gain_ref, g_ref,
    gq_ref, gk_ref, gv_ref, gg_ref,
    state, state_in, prefix, prefix_in,
    back, back_in, suffix, suffix_in,
    decay_out, decay_in,
    weight, weighted, attended, earlier_b, grad_att, part_k, part_v,
    norm_out, norm_in,
    gain_y_out, gain_y_in, gain_z_out, gain_z_in, gain_dp_out, gain_dp_in,
    decay_sems, state_send, state_recv, prefix_send, prefix_recv,
    back_send, back_recv, suffix_send, suffix_recv,
    norm_sems, gain_y_sems, gain_z_sems, gain_dp_sems,
):
    dp, me, tn = lax.axis_index("dp"), lax.axis_index("ctx"), lax.axis_index("tensor")
    z, y = me // RING, lax.rem(me, RING)
    scale = E ** (-0.5)
    full_width = TENSOR * HEADS * E

    def ctx_peer(i):
        return lax.rem(z + i // RING, RING) * RING + lax.rem(y + lax.rem(i, RING), RING)

    def tensor_peer(i):
        return lax.rem(tn + i, TENSOR)

    def y_peer(i):
        return z * RING + lax.rem(y + i, RING)

    def z_peer(i):
        return lax.rem(z + i, RING) * RING + y

    barrier = pltpu.get_barrier_semaphore()

    def greet_ctx(i, carry):
        pl.semaphore_signal(
            barrier, inc=1, device_id=(dp, ctx_peer(i), tn), device_id_type=MESH
        )
        return carry

    def greet_tensor(i, carry):
        pl.semaphore_signal(
            barrier, inc=1, device_id=(dp, me, tensor_peer(i)), device_id_type=MESH
        )
        return carry

    lax.fori_loop(1, CTX, greet_ctx, 0)
    lax.fori_loop(1, TENSOR, greet_tensor, 0)
    pl.semaphore_signal(barrier, inc=1, device_id=(1 - dp, me, tn), device_id_type=MESH)

    def remote(src, dst, send_sem, recv_sem, device):
        return pltpu.make_async_remote_copy(
            src_ref=src, dst_ref=dst, send_sem=send_sem, recv_sem=recv_sem,
            device_id=device, device_id_type=MESH,
        )

    def wait_bytes(ref, sem):
        pltpu.make_async_copy(ref, ref, sem).wait()

    def exchange(src, dst, send_sem, recv_sem):
        def go(i, carry):
            peer = ctx_peer(i)
            remote(src.at[peer], dst.at[me], send_sem, recv_sem, (dp, peer, tn)).start()
            return carry

        lax.fori_loop(1, CTX, go, 0)
        dst[me] = src[me]

    lanes = lax.broadcasted_iota(jnp.int32, (HEADS, E), 1)
    cumulative = f_ref[0]
    for shift in (1, 2, 4, 8, 16, 32, 64):
        moved = pltpu.roll(cumulative, shift, 1)
        cumulative = cumulative + jnp.where(lanes >= shift, moved, 0.0)
    block_decay = cumulative[:, E - 1 :]
    passing = jnp.broadcast_to(jnp.exp(-block_decay), (HEADS, E))
    for h in range(HEADS):
        decay_out[h % GROUP, h // GROUP] = passing[h]
    cumulative_t = cumulative.T
    query_decay = jnp.exp(-cumulative).T
    key_decay = jnp.exp(-(block_decay - cumulative)).T

    def columns(h):
        return slice(h * E, (h + 1) * E)

    def pieces(h):
        return h // GROUP, slice((h % GROUP) * OWNERS, (h % GROUP + 1) * OWNERS)

    def put_state(ref, h, value):
        batch, rows = pieces(h)
        ref[batch, rows] = value.reshape(OWNERS, 8, E)

    def get_state(ref, h):
        batch, rows = pieces(h)
        return ref[batch, rows].reshape(E, E)

    for h in range(HEADS):
        key_scaled = (k_ref[0, :, columns(h)].astype(F32) * key_decay[:, h : h + 1]).astype(BF16)
        put_state(state, h, matmul(key_scaled, v_ref[0, :, columns(h)], 0, 0))

    pl.semaphore_wait(barrier, CTX - 1 + TENSOR - 1 + 1)

    def send_decay(i, carry):
        peer = ctx_peer(i)
        remote(
            decay_out.at[peer // OWNERS], decay_in.at[me],
            decay_sems.at[0], decay_sems.at[1], (dp, peer, tn),
        ).start()
        return carry

    lax.fori_loop(1, CTX, send_decay, 0)
    decay_in[me] = decay_out[me // OWNERS]
    for b in range(BATCHES):
        exchange(state.at[b], state_in.at[b], state_send.at[b], state_recv.at[b])

    below = lax.broadcasted_iota(jnp.int32, (E, E), 0) >= lax.broadcasted_iota(
        jnp.int32, (E, E), 1
    )
    for h in range(HEADS):
        span = cumulative_t[:, h : h + 1] - cumulative[h : h + 1, :]
        now = jnp.where(below, jnp.exp(-jnp.where(below, span, 0.0)), 0.0)
        weight[h] = now
        scores = matmul(q_ref[0, :, columns(h)], k_ref[0, :, columns(h)], 1, 1)
        rounded = (scores * scale * now).astype(BF16)
        weighted[h] = rounded
        attended[h] = matmul(rounded, v_ref[0, :, columns(h)], 1, 0)

    others = pl.ds(0, CTX - 1)
    wait_bytes(decay_in.at[others], decay_sems.at[1])

    def run_scan(b, source, result, reverse):
        def step(i, total):
            at = CTX - 1 - i if reverse else i
            result[b, at] = total
            return total * decay_in[at, b : b + 1] + source[b, at]

        lax.fori_loop(0, CTX, step, jnp.zeros((8, E), F32), unroll=8)

    for b in range(BATCHES):
        wait_bytes(state_in.at[b, others], state_recv.at[b])
        run_scan(b, state_in, prefix, False)
        exchange(prefix.at[b], prefix_in.at[b], prefix_send.at[b], prefix_recv.at[b])

    squares = jnp.zeros((E, E), F32)
    products = jnp.zeros((E, E), F32)
    for b in range(BATCHES):
        wait_bytes(prefix_in.at[b, others], prefix_recv.at[b])
        for h in range(b * GROUP, (b + 1) * GROUP):
            state_b = get_state(prefix_in, h).astype(BF16)
            earlier_b[h] = state_b
            carried = matmul(q_ref[0, :, columns(h)], state_b, 1, 0)
            now = attended[h] + scale * query_decay[:, h : h + 1] * carried
            attended[h] = now
            grad_normed = g_ref[0, :, columns(h)].astype(F32) * gain_ref[h : h + 1, :]
            squares = squares + now * now
            products = products + grad_normed * now

    wide = lax.broadcasted_iota(jnp.int32, (E, E), 1)
    both = jnp.where(
        wide == 0,
        jnp.sum(squares, axis=1, keepdims=True),
        jnp.sum(products, axis=1, keepdims=True),
    ).T[0:8]
    norm_out[...] = both

    def send_norm(i, carry):
        remote(
            norm_out, norm_in.at[tn], norm_sems.at[0], norm_sems.at[1], (dp, me, tensor_peer(i))
        ).start()
        return carry

    lax.fori_loop(1, TENSOR, send_norm, 0)
    norm_in[tn] = both
    wait_bytes(norm_in.at[pl.ds(0, TENSOR - 1)], norm_sems.at[1])
    sums = (norm_in[0] + norm_in[1]) + (norm_in[2] + norm_in[3])
    inverse_rms = lax.rsqrt(sums[0:1] / full_width + EPSILON)
    projected = sums[1:2] * inverse_rms / full_width
    of_grad = jnp.broadcast_to(inverse_rms, (E, E)).T
    of_attended = jnp.broadcast_to(inverse_rms * inverse_rms * projected, (E, E)).T

    for b in range(BATCHES):
        for h in range(b * GROUP, (b + 1) * GROUP):
            grad_normed = g_ref[0, :, columns(h)].astype(F32) * gain_ref[h : h + 1, :]
            grad_now = (of_grad * grad_normed - of_attended * attended[h]).astype(BF16)
            grad_att[h] = grad_now
            query_scaled = (
                q_ref[0, :, columns(h)].astype(F32) * query_decay[:, h : h + 1]
            ).astype(BF16)
            put_state(back, h, matmul(query_scaled, grad_now, 0, 0))
        exchange(back.at[b], back_in.at[b], back_send.at[b], back_recv.at[b])

    for h in range(HEADS):
        normed = attended[h] * of_grad
        gain_y_out[h] = jnp.sum(g_ref[0, :, columns(h)].astype(F32) * normed, axis=0)

    def sum_ring(out, into, sems, peer_of, mine):
        def go(i, carry):
            remote(out, into.at[mine], sems.at[0], sems.at[1], (dp, peer_of(i), tn)).start()
            return carry

        lax.fori_loop(1, RING, go, 0)
        into[mine] = out[...]

    def ring_total(into, sems):
        wait_bytes(into.at[pl.ds(0, RING - 1)], sems.at[1])
        total = into[0]
        for i in range(1, RING):
            total = total + into[i]
        return total

    sum_ring(gain_y_out, gain_y_in, gain_y_sems, y_peer, y)

    for h in range(HEADS):
        grad_now = grad_att[h]
        scores = matmul(grad_now, v_ref[0, :, columns(h)], 1, 1)
        grad_weighted = (scores * scale * weight[h]).astype(BF16)
        grad_q = matmul(grad_weighted, k_ref[0, :, columns(h)], 1, 0) + scale * query_decay[
            :, h : h + 1
        ] * matmul(grad_now, earlier_b[h], 1, 1)
        gq_ref[0, :, columns(h)] = grad_q.astype(BF16)
        part_k[h] = matmul(grad_weighted, q_ref[0, :, columns(h)], 0, 0)
        part_v[h] = matmul(weighted[h], grad_now, 0, 0)

    for b in range(BATCHES):
        wait_bytes(back_in.at[b, others], back_recv.at[b])
        run_scan(b, back_in, suffix, True)
        exchange(suffix.at[b], suffix_in.at[b], suffix_send.at[b], suffix_recv.at[b])

    gain_z_out[...] = ring_total(gain_y_in, gain_y_sems)
    sum_ring(gain_z_out, gain_z_in, gain_z_sems, z_peer, z)
    gain_total = ring_total(gain_z_in, gain_z_sems)
    gain_dp_out[...] = gain_total
    other_core = remote(
        gain_dp_out, gain_dp_in, gain_dp_sems.at[0], gain_dp_sems.at[1], (1 - dp, me, tn)
    )
    other_core.start()

    for b in range(BATCHES):
        wait_bytes(suffix_in.at[b, others], suffix_recv.at[b])
        for h in range(b * GROUP, (b + 1) * GROUP):
            later_b = get_state(suffix_in, h).astype(BF16)
            scaling = scale * key_decay[:, h : h + 1]
            grad_k = part_k[h] + scaling * matmul(v_ref[0, :, columns(h)], later_b, 1, 1)
            grad_v = part_v[h] + scaling * matmul(k_ref[0, :, columns(h)], later_b, 1, 0)
            gk_ref[0, :, columns(h)] = grad_k.astype(BF16)
            gv_ref[0, :, columns(h)] = grad_v.astype(BF16)

    other_core.wait()
    gg_ref[...] = gain_total + gain_dp_in[...]

    wait_bytes(decay_in.at[others], decay_sems.at[0])
    for b in range(BATCHES):
        wait_bytes(state.at[b, others], state_send.at[b])
        wait_bytes(prefix.at[b, others], prefix_send.at[b])
        wait_bytes(back.at[b, others], back_send.at[b])
        wait_bytes(suffix.at[b, others], suffix_send.at[b])
    wait_bytes(norm_in.at[pl.ds(0, TENSOR - 1)], norm_sems.at[0])
    wait_bytes(gain_y_in.at[pl.ds(0, RING - 1)], gain_y_sems.at[0])
    wait_bytes(gain_z_in.at[pl.ds(0, RING - 1)], gain_z_sems.at[0])


def shards(queries, keys, values, forget, gain, grad_out):
    block = jax.ShapeDtypeStruct(queries.shape, BF16)
    states = pltpu.VMEM((BATCHES, CTX, 8, E), F32)
    squares_f32 = pltpu.VMEM((HEADS, E, E), F32)
    squares_bf16 = pltpu.VMEM((HEADS, E, E), BF16)
    tile = pltpu.VMEM((8, E), F32)
    ring = pltpu.VMEM((RING, 8, E), F32)
    pair = pltpu.SemaphoreType.DMA((2,))
    vmem = pl.BlockSpec(memory_space=pltpu.VMEM)
    grad_q, grad_k, grad_v, grad_gain = pl.pallas_call(
        kernel,
        out_shape=(block, block, block, jax.ShapeDtypeStruct((HEADS, E), F32)),
        in_specs=[vmem] * 6,
        out_specs=(vmem,) * 4,
        scratch_shapes=[states] * 8
        + [pltpu.VMEM((GROUP, BATCHES, E), F32), pltpu.VMEM((CTX, BATCHES, E), F32)]
        + [squares_f32, squares_bf16, squares_f32, squares_bf16, squares_bf16]
        + [squares_f32, squares_f32]
        + [tile, pltpu.VMEM((TENSOR, 8, E), F32)]
        + [tile, ring, tile, ring, tile, tile]
        + [pair] * 13,
        compiler_params=pltpu.CompilerParams(
            collective_id=0, has_side_effects=True, vmem_limit_bytes=40 << 20
        ),
    )(queries, keys, values, forget, gain.reshape(HEADS, E), grad_out)
    return grad_q, grad_k, grad_v, grad_gain.reshape(-1)


def solution(mesh):
    in_specs = (
        P("dp", "ctx", "tensor"),
        P("dp", "ctx", "tensor"),
        P("dp", "ctx", "tensor"),
        P("dp", "tensor", "ctx"),
        P("tensor"),
        P("dp", "ctx", "tensor"),
    )
    out_specs = (
        P("dp", "ctx", "tensor"),
        P("dp", "ctx", "tensor"),
        P("dp", "ctx", "tensor"),
        P("tensor"),
    )
    return jax.shard_map(shards, mesh=mesh, in_specs=in_specs, out_specs=out_specs, check_vma=False)
```

```python
import functools

import jax
import jax.numpy as jnp
from jax import lax
from jax.experimental import pallas as pl
from jax.experimental.pallas import tpu as pltpu
from jax.sharding import PartitionSpec as P

E = 128
EPSILON = 1e-05
MESH = pl.DeviceIdType.MESH
F32 = jnp.float32
BF16 = jnp.bfloat16

HEADS = 8
CTX = 64
RING = 8
TENSOR = 4
BATCHES = 2
GROUP = HEADS // BATCHES
OWNERS = CTX // GROUP


def matmul(a, b, contract_a, contract_b):
    return lax.dot_general(
        a, b, (((contract_a,), (contract_b,)), ((), ())), preferred_element_type=F32
    )


def kernel(
    q_hbm, k_hbm, v_hbm, f_hbm, gain_hbm, g_hbm,
    gq_ref, gk_ref, gv_ref, gg_ref,
    q_ref, k_ref, v_ref, f_ref, gain_ref, g_ref,
    state, state_in, prefix, prefix_in,
    back, back_in, suffix, suffix_in,
    decay_out, decay_in,
    weight, weighted, attended, earlier_b, grad_att, part_k, part_v,
    norm_out, norm_in,
    gain_y_out, gain_y_in, gain_z_out, gain_z_in, gain_dp_out, gain_dp_in,
    decay_sems, state_send, state_recv, prefix_send, prefix_recv,
    back_send, back_recv, suffix_send, suffix_recv,
    norm_sems, gain_y_sems, gain_z_sems, gain_dp_sems, load_sems,
):
    dp, me, tn = lax.axis_index("dp"), lax.axis_index("ctx"), lax.axis_index("tensor")
    z, y = me // RING, lax.rem(me, RING)
    scale = E ** (-0.5)
    full_width = TENSOR * HEADS * E

    def ctx_peer(i):
        return lax.rem(z + i // RING, RING) * RING + lax.rem(y + lax.rem(i, RING), RING)

    def tensor_peer(i):
        return lax.rem(tn + i, TENSOR)

    def y_peer(i):
        return z * RING + lax.rem(y + i, RING)

    def z_peer(i):
        return lax.rem(z + i, RING) * RING + y

    loads = [
        pltpu.make_async_copy(source, target, load_sems.at[i])
        for i, (source, target) in enumerate(
            (
                (f_hbm, f_ref), (k_hbm, k_ref), (v_hbm, v_ref),
                (q_hbm, q_ref), (g_hbm, g_ref), (gain_hbm, gain_ref),
            )
        )
    ]
    for load in loads:
        load.start()

    barrier = pltpu.get_barrier_semaphore()

    def greet_ctx(i, carry):
        pl.semaphore_signal(
            barrier, inc=1, device_id=(dp, ctx_peer(i), tn), device_id_type=MESH
        )
        return carry

    def greet_tensor(i, carry):
        pl.semaphore_signal(
            barrier, inc=1, device_id=(dp, me, tensor_peer(i)), device_id_type=MESH
        )
        return carry

    lax.fori_loop(1, CTX, greet_ctx, 0)
    lax.fori_loop(1, TENSOR, greet_tensor, 0)
    pl.semaphore_signal(barrier, inc=1, device_id=(1 - dp, me, tn), device_id_type=MESH)

    def remote(src, dst, send_sem, recv_sem, device):
        return pltpu.make_async_remote_copy(
            src_ref=src, dst_ref=dst, send_sem=send_sem, recv_sem=recv_sem,
            device_id=device, device_id_type=MESH,
        )

    def wait_bytes(ref, sem):
        pltpu.make_async_copy(ref, ref, sem).wait()

    def exchange(src, dst, send_sem, recv_sem):
        def go(i, carry):
            peer = ctx_peer(i)
            remote(src.at[peer], dst.at[me], send_sem, recv_sem, (dp, peer, tn)).start()
            return carry

        lax.fori_loop(1, CTX, go, 0)
        dst[me] = src[me]

    loads[0].wait()
    lanes = lax.broadcasted_iota(jnp.int32, (HEADS, E), 1)
    cumulative = f_ref[0]
    for shift in (1, 2, 4, 8, 16, 32, 64):
        moved = pltpu.roll(cumulative, shift, 1)
        cumulative = cumulative + jnp.where(lanes >= shift, moved, 0.0)
    block_decay = cumulative[:, E - 1 :]
    passing = jnp.broadcast_to(jnp.exp(-block_decay), (HEADS, E))
    for h in range(HEADS):
        decay_out[h % GROUP, h // GROUP] = passing[h]
    cumulative_t = cumulative.T
    query_decay = jnp.exp(-cumulative).T
    key_decay = jnp.exp(-(block_decay - cumulative)).T

    def columns(h):
        return slice(h * E, (h + 1) * E)

    def pieces(h):
        return h // GROUP, slice((h % GROUP) * OWNERS, (h % GROUP + 1) * OWNERS)

    def put_state(ref, h, value):
        batch, rows = pieces(h)
        ref[batch, rows] = value.reshape(OWNERS, 8, E)

    def get_state(ref, h):
        batch, rows = pieces(h)
        return ref[batch, rows].reshape(E, E)

    loads[1].wait()
    loads[2].wait()
    for h in range(HEADS):
        key_scaled = (k_ref[0, :, columns(h)].astype(F32) * key_decay[:, h : h + 1]).astype(BF16)
        put_state(state, h, matmul(key_scaled, v_ref[0, :, columns(h)], 0, 0))

    pl.semaphore_wait(barrier, CTX - 1 + TENSOR - 1 + 1)

    def send_decay(i, carry):
        peer = ctx_peer(i)
        remote(
            decay_out.at[peer // OWNERS], decay_in.at[me],
            decay_sems.at[0], decay_sems.at[1], (dp, peer, tn),
        ).start()
        return carry

    exchange(state.at[0], state_in.at[0], state_send.at[0], state_recv.at[0])
    lax.fori_loop(1, CTX, send_decay, 0)
    decay_in[me] = decay_out[me // OWNERS]
    for b in range(1, BATCHES):
        exchange(state.at[b], state_in.at[b], state_send.at[b], state_recv.at[b])
    for load in loads[3:]:
        load.wait()

    below = lax.broadcasted_iota(jnp.int32, (E, E), 0) >= lax.broadcasted_iota(
        jnp.int32, (E, E), 1
    )
    for h in range(HEADS):
        span = cumulative_t[:, h : h + 1] - cumulative[h : h + 1, :]
        now = jnp.where(below, jnp.exp(-jnp.where(below, span, 0.0)), 0.0)
        weight[h] = now
        scores = matmul(q_ref[0, :, columns(h)], k_ref[0, :, columns(h)], 1, 1)
        rounded = (scores * scale * now).astype(BF16)
        weighted[h] = rounded
        attended[h] = matmul(rounded, v_ref[0, :, columns(h)], 1, 0)

    others = pl.ds(0, CTX - 1)
    wait_bytes(decay_in.at[others], decay_sems.at[1])

    def run_scan(b, source, result, reverse):
        def step(i, total):
            at = CTX - 1 - i if reverse else i
            result[b, at] = total
            return total * decay_in[at, b : b + 1] + source[b, at]

        lax.fori_loop(0, CTX, step, jnp.zeros((8, E), F32), unroll=8)

    for b in range(BATCHES):
        wait_bytes(state_in.at[b, others], state_recv.at[b])
        run_scan(b, state_in, prefix, False)
        exchange(prefix.at[b], prefix_in.at[b], prefix_send.at[b], prefix_recv.at[b])

    squares = jnp.zeros((E, E), F32)
    products = jnp.zeros((E, E), F32)
    for b in range(BATCHES):
        wait_bytes(prefix_in.at[b, others], prefix_recv.at[b])
        for h in range(b * GROUP, (b + 1) * GROUP):
            state_b = get_state(prefix_in, h).astype(BF16)
            earlier_b[h] = state_b
            carried = matmul(q_ref[0, :, columns(h)], state_b, 1, 0)
            now = attended[h] + scale * query_decay[:, h : h + 1] * carried
            attended[h] = now
            grad_normed = g_ref[0, :, columns(h)].astype(F32) * gain_ref[h : h + 1, :]
            squares = squares + now * now
            products = products + grad_normed * now

    wide = lax.broadcasted_iota(jnp.int32, (E, E), 1)
    both = jnp.where(
        wide == 0,
        jnp.sum(squares, axis=1, keepdims=True),
        jnp.sum(products, axis=1, keepdims=True),
    ).T[0:8]
    norm_out[...] = both

    def send_norm(i, carry):
        remote(
            norm_out, norm_in.at[tn], norm_sems.at[0], norm_sems.at[1], (dp, me, tensor_peer(i))
        ).start()
        return carry

    lax.fori_loop(1, TENSOR, send_norm, 0)
    norm_in[tn] = both
    wait_bytes(norm_in.at[pl.ds(0, TENSOR - 1)], norm_sems.at[1])
    sums = (norm_in[0] + norm_in[1]) + (norm_in[2] + norm_in[3])
    inverse_rms = lax.rsqrt(sums[0:1] / full_width + EPSILON)
    projected = sums[1:2] * inverse_rms / full_width
    of_grad = jnp.broadcast_to(inverse_rms, (E, E)).T
    of_attended = jnp.broadcast_to(inverse_rms * inverse_rms * projected, (E, E)).T

    for b in range(BATCHES):
        for h in range(b * GROUP, (b + 1) * GROUP):
            grad_normed = g_ref[0, :, columns(h)].astype(F32) * gain_ref[h : h + 1, :]
            grad_now = (of_grad * grad_normed - of_attended * attended[h]).astype(BF16)
            grad_att[h] = grad_now
            query_scaled = (
                q_ref[0, :, columns(h)].astype(F32) * query_decay[:, h : h + 1]
            ).astype(BF16)
            put_state(back, h, matmul(query_scaled, grad_now, 0, 0))
        exchange(back.at[b], back_in.at[b], back_send.at[b], back_recv.at[b])

    for h in range(HEADS):
        normed = attended[h] * of_grad
        gain_y_out[h] = jnp.sum(g_ref[0, :, columns(h)].astype(F32) * normed, axis=0)

    def sum_ring(out, into, sems, peer_of, mine):
        def go(i, carry):
            remote(out, into.at[mine], sems.at[0], sems.at[1], (dp, peer_of(i), tn)).start()
            return carry

        lax.fori_loop(1, RING, go, 0)
        into[mine] = out[...]

    def ring_total(into, sems):
        wait_bytes(into.at[pl.ds(0, RING - 1)], sems.at[1])
        total = into[0]
        for i in range(1, RING):
            total = total + into[i]
        return total

    sum_ring(gain_y_out, gain_y_in, gain_y_sems, y_peer, y)

    for h in range(HEADS):
        grad_now = grad_att[h]
        scores = matmul(grad_now, v_ref[0, :, columns(h)], 1, 1)
        grad_weighted = (scores * scale * weight[h]).astype(BF16)
        grad_q = matmul(grad_weighted, k_ref[0, :, columns(h)], 1, 0) + scale * query_decay[
            :, h : h + 1
        ] * matmul(grad_now, earlier_b[h], 1, 1)
        gq_ref[0, :, columns(h)] = grad_q.astype(BF16)
        part_k[h] = matmul(grad_weighted, q_ref[0, :, columns(h)], 0, 0)
        part_v[h] = matmul(weighted[h], grad_now, 0, 0)

    for b in range(BATCHES):
        wait_bytes(back_in.at[b, others], back_recv.at[b])
        run_scan(b, back_in, suffix, True)
        exchange(suffix.at[b], suffix_in.at[b], suffix_send.at[b], suffix_recv.at[b])

    gain_z_out[...] = ring_total(gain_y_in, gain_y_sems)
    sum_ring(gain_z_out, gain_z_in, gain_z_sems, z_peer, z)
    gain_total = ring_total(gain_z_in, gain_z_sems)
    gain_dp_out[...] = gain_total
    other_core = remote(
        gain_dp_out, gain_dp_in, gain_dp_sems.at[0], gain_dp_sems.at[1], (1 - dp, me, tn)
    )
    other_core.start()

    for b in range(BATCHES):
        wait_bytes(suffix_in.at[b, others], suffix_recv.at[b])
        for h in range(b * GROUP, (b + 1) * GROUP):
            later_b = get_state(suffix_in, h).astype(BF16)
            scaling = scale * key_decay[:, h : h + 1]
            grad_k = part_k[h] + scaling * matmul(v_ref[0, :, columns(h)], later_b, 1, 1)
            grad_v = part_v[h] + scaling * matmul(k_ref[0, :, columns(h)], later_b, 1, 0)
            gk_ref[0, :, columns(h)] = grad_k.astype(BF16)
            gv_ref[0, :, columns(h)] = grad_v.astype(BF16)

    other_core.wait()
    gg_ref[...] = gain_total + gain_dp_in[...]

    wait_bytes(decay_in.at[others], decay_sems.at[0])
    for b in range(BATCHES):
        wait_bytes(state.at[b, others], state_send.at[b])
        wait_bytes(prefix.at[b, others], prefix_send.at[b])
        wait_bytes(back.at[b, others], back_send.at[b])
        wait_bytes(suffix.at[b, others], suffix_send.at[b])
    wait_bytes(norm_in.at[pl.ds(0, TENSOR - 1)], norm_sems.at[0])
    wait_bytes(gain_y_in.at[pl.ds(0, RING - 1)], gain_y_sems.at[0])
    wait_bytes(gain_z_in.at[pl.ds(0, RING - 1)], gain_z_sems.at[0])


def store(*refs):
    sources, targets, sems = refs[:4], refs[4:8], refs[8]
    copies = [
        pltpu.make_async_copy(source, target, sems.at[i])
        for i, (source, target) in enumerate(zip(sources, targets))
    ]
    for copy in copies:
        copy.start()
    for copy in copies:
        copy.wait()


def shards(queries, keys, values, forget, gain, grad_out):
    block = jax.ShapeDtypeStruct(queries.shape, BF16)
    states = pltpu.VMEM((BATCHES, CTX, 8, E), F32)
    squares_f32 = pltpu.VMEM((HEADS, E, E), F32)
    squares_bf16 = pltpu.VMEM((HEADS, E, E), BF16)
    tile = pltpu.VMEM((8, E), F32)
    ring = pltpu.VMEM((RING, 8, E), F32)
    pair = pltpu.SemaphoreType.DMA((2,))
    vmem = pl.BlockSpec(memory_space=pltpu.VMEM)
    hbm = pl.BlockSpec(memory_space=pltpu.HBM)
    tokens = pltpu.VMEM(queries.shape, BF16)
    shapes = (block, block, block, jax.ShapeDtypeStruct((HEADS, E), F32))
    grads = pl.pallas_call(
        kernel,
        out_shape=shapes,
        in_specs=[hbm] * 6,
        out_specs=(vmem,) * 4,
        scratch_shapes=[tokens, tokens, tokens, pltpu.VMEM(forget.shape, F32), tile, tokens]
        + [states] * 8
        + [pltpu.VMEM((GROUP, BATCHES, E), F32), pltpu.VMEM((CTX, BATCHES, E), F32)]
        + [squares_f32, squares_bf16, squares_f32, squares_bf16, squares_bf16]
        + [squares_f32, squares_f32]
        + [tile, pltpu.VMEM((TENSOR, 8, E), F32)]
        + [tile, ring, tile, ring, tile, tile]
        + [pair] * 13
        + [pltpu.SemaphoreType.DMA((6,))],
        compiler_params=pltpu.CompilerParams(
            collective_id=0, has_side_effects=True, vmem_limit_bytes=40 << 20
        ),
    )(
        *(
            pltpu.with_memory_space_constraint(x, pltpu.HBM)
            for x in (queries, keys, values, forget, gain.reshape(HEADS, E), grad_out)
        )
    )
    grad_q, grad_k, grad_v, grad_gain = pl.pallas_call(
        store,
        out_shape=shapes,
        in_specs=[vmem] * 4,
        out_specs=(hbm,) * 4,
        scratch_shapes=[pltpu.SemaphoreType.DMA((4,))],
    )(*grads)
    return grad_q, grad_k, grad_v, grad_gain.reshape(-1)


def solution(mesh):
    in_specs = (
        P("dp", "ctx", "tensor"),
        P("dp", "ctx", "tensor"),
        P("dp", "ctx", "tensor"),
        P("dp", "tensor", "ctx"),
        P("tensor"),
        P("dp", "ctx", "tensor"),
    )
    out_specs = (
        P("dp", "ctx", "tensor"),
        P("dp", "ctx", "tensor"),
        P("dp", "ctx", "tensor"),
        P("tensor"),
    )
    return jax.shard_map(shards, mesh=mesh, in_specs=in_specs, out_specs=out_specs, check_vma=False)
```

```python
import functools

import jax
import jax.numpy as jnp
from jax import lax
from jax.experimental import pallas as pl
from jax.experimental.pallas import tpu as pltpu
from jax.sharding import PartitionSpec as P

E = 128
EPSILON = 1e-05
MESH = pl.DeviceIdType.MESH
F32 = jnp.float32
BF16 = jnp.bfloat16

HEADS = 8
CTX = 64
RING = 8
TENSOR = 4
BATCHES = 2
GROUP = HEADS // BATCHES
OWNERS = CTX // GROUP


def matmul(a, b, contract_a, contract_b):
    return lax.dot_general(
        a, b, (((contract_a,), (contract_b,)), ((), ())), preferred_element_type=F32
    )


def kernel(
    q_hbm, k_hbm, v_hbm, f_hbm, gain_hbm, g_hbm,
    gq_ref, gk_ref, gv_ref, gg_ref,
    q_ref, k_ref, v_ref, f_ref, gain_ref, g_ref,
    state, state_in, prefix, prefix_in,
    back, back_in, suffix, suffix_in,
    decay_out, decay_in,
    weight, weighted, attended, earlier_b, grad_att, part_k, part_v,
    grad_normed, of_query, of_key, query_scaled,
    norm_out, norm_in,
    gain_y_out, gain_y_in, gain_z_out, gain_z_in, gain_dp_out, gain_dp_in,
    decay_sems, state_send, state_recv, prefix_send, prefix_recv,
    back_send, back_recv, suffix_send, suffix_recv,
    norm_sems, gain_y_sems, gain_z_sems, gain_dp_sems, load_sems,
):
    dp, me, tn = lax.axis_index("dp"), lax.axis_index("ctx"), lax.axis_index("tensor")
    z, y = me // RING, lax.rem(me, RING)
    scale = E ** (-0.5)
    full_width = TENSOR * HEADS * E

    def alternate(i):
        half, odd = i // 2, lax.rem(i, 2)
        return half + odd * (RING - 1 - 2 * half)

    def ctx_peer(i):
        i = CTX - i
        to_z, to_y = alternate(i // RING), alternate(lax.rem(i, RING))
        return lax.rem(z + to_z, RING) * RING + lax.rem(y + to_y, RING)

    def tensor_peer(i):
        return lax.rem(tn + i, TENSOR)

    def y_peer(i):
        return z * RING + lax.rem(y + i, RING)

    def z_peer(i):
        return lax.rem(z + i, RING) * RING + y

    loads = [
        pltpu.make_async_copy(source, target, load_sems.at[i])
        for i, (source, target) in enumerate(
            (
                (f_hbm, f_ref), (k_hbm, k_ref), (v_hbm, v_ref),
                (q_hbm, q_ref), (g_hbm, g_ref), (gain_hbm, gain_ref),
            )
        )
    ]
    for load in loads:
        load.start()

    barrier = pltpu.get_barrier_semaphore()

    def greet_ctx(i, carry):
        pl.semaphore_signal(
            barrier, inc=1, device_id=(dp, ctx_peer(i), tn), device_id_type=MESH
        )
        return carry

    def greet_tensor(i, carry):
        pl.semaphore_signal(
            barrier, inc=1, device_id=(dp, me, tensor_peer(i)), device_id_type=MESH
        )
        return carry

    lax.fori_loop(1, CTX, greet_ctx, 0)
    lax.fori_loop(1, TENSOR, greet_tensor, 0)
    pl.semaphore_signal(barrier, inc=1, device_id=(1 - dp, me, tn), device_id_type=MESH)

    def remote(src, dst, send_sem, recv_sem, device):
        return pltpu.make_async_remote_copy(
            src_ref=src, dst_ref=dst, send_sem=send_sem, recv_sem=recv_sem,
            device_id=device, device_id_type=MESH,
        )

    def wait_bytes(ref, sem):
        pltpu.make_async_copy(ref, ref, sem).wait()

    def exchange(src, dst, send_sem, recv_sem):
        def go(i, carry):
            peer = ctx_peer(i)
            remote(src.at[peer], dst.at[me], send_sem, recv_sem, (dp, peer, tn)).start()
            return carry

        lax.fori_loop(1, CTX, go, 0)
        dst[me] = src[me]

    loads[0].wait()
    lanes = lax.broadcasted_iota(jnp.int32, (HEADS, E), 1)
    cumulative = f_ref[0]
    for shift in (1, 2, 4, 8, 16, 32, 64):
        moved = pltpu.roll(cumulative, shift, 1)
        cumulative = cumulative + jnp.where(lanes >= shift, moved, 0.0)
    block_decay = cumulative[:, E - 1 :]
    passing = jnp.broadcast_to(jnp.exp(-block_decay), (HEADS, E))
    for h in range(HEADS):
        decay_out[h % GROUP, h // GROUP] = passing[h]
    cumulative_t = cumulative.T
    query_decay = jnp.exp(-cumulative).T
    key_decay = jnp.exp(-(block_decay - cumulative)).T

    def columns(h):
        return slice(h * E, (h + 1) * E)

    def pieces(h):
        return h // GROUP, slice((h % GROUP) * OWNERS, (h % GROUP + 1) * OWNERS)

    def put_state(ref, h, value):
        batch, rows = pieces(h)
        ref[batch, rows] = value.reshape(OWNERS, 8, E)

    def get_state(ref, h):
        batch, rows = pieces(h)
        return ref[batch, rows].reshape(E, E)

    loads[1].wait()
    loads[2].wait()

    def make_state(h):
        key_scaled = (k_ref[0, :, columns(h)].astype(F32) * key_decay[:, h : h + 1]).astype(BF16)
        put_state(state, h, matmul(key_scaled, v_ref[0, :, columns(h)], 0, 0))

    for h in range(GROUP):
        make_state(h)
    pl.semaphore_wait(barrier, CTX - 1 + TENSOR - 1 + 1)

    def send_decay(i, carry):
        peer = ctx_peer(i)
        remote(
            decay_out.at[peer // OWNERS], decay_in.at[me],
            decay_sems.at[0], decay_sems.at[1], (dp, peer, tn),
        ).start()
        return carry

    exchange(state.at[0], state_in.at[0], state_send.at[0], state_recv.at[0])
    lax.fori_loop(1, CTX, send_decay, 0)
    decay_in[me] = decay_out[me // OWNERS]
    for h in range(GROUP, HEADS):
        make_state(h)
    exchange(state.at[1], state_in.at[1], state_send.at[1], state_recv.at[1])
    for load in loads[3:]:
        load.wait()

    below = lax.broadcasted_iota(jnp.int32, (E, E), 0) >= lax.broadcasted_iota(
        jnp.int32, (E, E), 1
    )

    def make_local(h):
        span = cumulative_t[:, h : h + 1] - cumulative[h : h + 1, :]
        now = jnp.where(below, jnp.exp(-jnp.where(below, span, 0.0)), 0.0)
        weight[h] = now
        scores = matmul(q_ref[0, :, columns(h)], k_ref[0, :, columns(h)], 1, 1)
        rounded = (scores * scale * now).astype(BF16)
        weighted[h] = rounded
        attended[h] = matmul(rounded, v_ref[0, :, columns(h)], 1, 0)
        grad_normed[h] = g_ref[0, :, columns(h)].astype(F32) * gain_ref[h : h + 1, :]
        of_query[h] = jnp.broadcast_to(scale * query_decay[:, h : h + 1], (E, E))
        of_key[h] = jnp.broadcast_to(scale * key_decay[:, h : h + 1], (E, E))
        scaled = q_ref[0, :, columns(h)].astype(F32) * query_decay[:, h : h + 1]
        query_scaled[h] = scaled.T.astype(BF16)

    for h in range(GROUP):
        make_local(h)

    others = pl.ds(0, CTX - 1)
    wait_bytes(decay_in.at[others], decay_sems.at[1])

    def run_scan(b, source, result, reverse):
        def step(i, total):
            at = CTX - 1 - i if reverse else i
            result[b, at] = total
            return total * decay_in[at, b : b + 1] + source[b, at]

        lax.fori_loop(0, CTX, step, jnp.zeros((8, E), F32), unroll=8)

    for b in range(BATCHES):
        wait_bytes(state_in.at[b, others], state_recv.at[b])
        run_scan(b, state_in, prefix, False)
        exchange(prefix.at[b], prefix_in.at[b], prefix_send.at[b], prefix_recv.at[b])
        for h in range(GROUP + 2 * b, GROUP + 2 * b + 2):
            make_local(h)

    squares = jnp.zeros((E, E), F32)
    products = jnp.zeros((E, E), F32)
    for b in range(BATCHES):
        wait_bytes(prefix_in.at[b, others], prefix_recv.at[b])
        for h in range(b * GROUP, (b + 1) * GROUP):
            state_b = get_state(prefix_in, h).astype(BF16)
            earlier_b[h] = state_b
            carried = matmul(q_ref[0, :, columns(h)], state_b, 1, 0)
            now = attended[h] + of_query[h] * carried
            attended[h] = now
            squares = squares + now * now
            products = products + grad_normed[h] * now

    wide = lax.broadcasted_iota(jnp.int32, (E, E), 1)
    both = jnp.where(
        wide == 0,
        jnp.sum(squares, axis=1, keepdims=True),
        jnp.sum(products, axis=1, keepdims=True),
    ).T[0:8]
    norm_out[...] = both

    def send_norm(i, carry):
        remote(
            norm_out, norm_in.at[tn], norm_sems.at[0], norm_sems.at[1], (dp, me, tensor_peer(i))
        ).start()
        return carry

    lax.fori_loop(1, TENSOR, send_norm, 0)
    norm_in[tn] = both
    wait_bytes(norm_in.at[pl.ds(0, TENSOR - 1)], norm_sems.at[1])
    sums = (norm_in[0] + norm_in[1]) + (norm_in[2] + norm_in[3])
    inverse_rms = lax.rsqrt(sums[0:1] / full_width + EPSILON)
    projected = sums[1:2] * inverse_rms / full_width
    of_grad = jnp.broadcast_to(inverse_rms, (E, E)).T
    of_attended = jnp.broadcast_to(inverse_rms * inverse_rms * projected, (E, E)).T

    def make_back(b):
        for h in range(b * GROUP, (b + 1) * GROUP):
            grad_now = (of_grad * grad_normed[h] - of_attended * attended[h]).astype(BF16)
            grad_att[h] = grad_now
            put_state(back, h, matmul(query_scaled[h], grad_now, 1, 0))
        exchange(back.at[b], back_in.at[b], back_send.at[b], back_recv.at[b])

    def sum_ring(out, into, sems, peer_of, mine):
        def go(i, carry):
            remote(out, into.at[mine], sems.at[0], sems.at[1], (dp, peer_of(i), tn)).start()
            return carry

        lax.fori_loop(1, RING, go, 0)
        into[mine] = out[...]

    def ring_total(into, sems):
        wait_bytes(into.at[pl.ds(0, RING - 1)], sems.at[1])
        total = into[0]
        for i in range(1, RING):
            total = total + into[i]
        return total

    make_back(0)
    for h in range(HEADS):
        normed = attended[h] * of_grad
        gain_y_out[h] = jnp.sum(g_ref[0, :, columns(h)].astype(F32) * normed, axis=0)
    sum_ring(gain_y_out, gain_y_in, gain_y_sems, y_peer, y)
    make_back(1)

    def make_parts(h):
        grad_now = grad_att[h]
        scores = matmul(grad_now, v_ref[0, :, columns(h)], 1, 1)
        grad_weighted = (scores * scale * weight[h]).astype(BF16)
        grad_q = matmul(grad_weighted, k_ref[0, :, columns(h)], 1, 0) + of_query[h] * matmul(
            grad_now, earlier_b[h], 1, 1
        )
        gq_ref[0, :, columns(h)] = grad_q.astype(BF16)
        part_k[h] = matmul(grad_weighted, q_ref[0, :, columns(h)], 0, 0)
        part_v[h] = matmul(weighted[h], grad_now, 0, 0)

    for h in range(GROUP):
        make_parts(h)

    gain_z_out[...] = ring_total(gain_y_in, gain_y_sems)
    sum_ring(gain_z_out, gain_z_in, gain_z_sems, z_peer, z)
    other_core = remote(
        gain_dp_out, gain_dp_in, gain_dp_sems.at[0], gain_dp_sems.at[1], (1 - dp, me, tn)
    )
    for b in range(BATCHES):
        wait_bytes(back_in.at[b, others], back_recv.at[b])
        run_scan(b, back_in, suffix, True)
        if b == BATCHES - 1:
            gain_total = ring_total(gain_z_in, gain_z_sems)
            gain_dp_out[...] = gain_total
            other_core.start()
        exchange(suffix.at[b], suffix_in.at[b], suffix_send.at[b], suffix_recv.at[b])
        for h in range(GROUP + 2 * b, GROUP + 2 * b + 2):
            make_parts(h)

    for b in range(BATCHES):
        wait_bytes(suffix_in.at[b, others], suffix_recv.at[b])
        for h in range(b * GROUP, (b + 1) * GROUP):
            later_b = get_state(suffix_in, h).astype(BF16)
            grad_k = part_k[h] + of_key[h] * matmul(v_ref[0, :, columns(h)], later_b, 1, 1)
            grad_v = part_v[h] + of_key[h] * matmul(k_ref[0, :, columns(h)], later_b, 1, 0)
            gk_ref[0, :, columns(h)] = grad_k.astype(BF16)
            gv_ref[0, :, columns(h)] = grad_v.astype(BF16)

    other_core.wait()
    gg_ref[...] = gain_total + gain_dp_in[...]

    wait_bytes(decay_in.at[others], decay_sems.at[0])
    for b in range(BATCHES):
        wait_bytes(state.at[b, others], state_send.at[b])
        wait_bytes(prefix.at[b, others], prefix_send.at[b])
        wait_bytes(back.at[b, others], back_send.at[b])
        wait_bytes(suffix.at[b, others], suffix_send.at[b])
    wait_bytes(norm_in.at[pl.ds(0, TENSOR - 1)], norm_sems.at[0])
    wait_bytes(gain_y_in.at[pl.ds(0, RING - 1)], gain_y_sems.at[0])
    wait_bytes(gain_z_in.at[pl.ds(0, RING - 1)], gain_z_sems.at[0])


def store(*refs):
    sources, targets, sems = refs[:4], refs[4:8], refs[8]
    copies = [
        pltpu.make_async_copy(source, target, sems.at[i])
        for i, (source, target) in enumerate(zip(sources, targets))
    ]
    for copy in copies:
        copy.start()
    for copy in copies:
        copy.wait()


def shards(queries, keys, values, forget, gain, grad_out):
    block = jax.ShapeDtypeStruct(queries.shape, BF16)
    states = pltpu.VMEM((BATCHES, CTX, 8, E), F32)
    squares_f32 = pltpu.VMEM((HEADS, E, E), F32)
    squares_bf16 = pltpu.VMEM((HEADS, E, E), BF16)
    tile = pltpu.VMEM((8, E), F32)
    ring = pltpu.VMEM((RING, 8, E), F32)
    pair = pltpu.SemaphoreType.DMA((2,))
    vmem = pl.BlockSpec(memory_space=pltpu.VMEM)
    hbm = pl.BlockSpec(memory_space=pltpu.HBM)
    tokens = pltpu.VMEM(queries.shape, BF16)
    shapes = (block, block, block, jax.ShapeDtypeStruct((HEADS, E), F32))
    grads = pl.pallas_call(
        kernel,
        out_shape=shapes,
        in_specs=[hbm] * 6,
        out_specs=(vmem,) * 4,
        scratch_shapes=[tokens, tokens, tokens, pltpu.VMEM(forget.shape, F32), tile, tokens]
        + [states] * 8
        + [pltpu.VMEM((GROUP, BATCHES, E), F32), pltpu.VMEM((CTX, BATCHES, E), F32)]
        + [squares_f32, squares_bf16, squares_f32, squares_bf16, squares_bf16]
        + [squares_f32] * 5
        + [squares_bf16]
        + [tile, pltpu.VMEM((TENSOR, 8, E), F32)]
        + [tile, ring, tile, ring, tile, tile]
        + [pair] * 13
        + [pltpu.SemaphoreType.DMA((6,))],
        compiler_params=pltpu.CompilerParams(
            collective_id=0, has_side_effects=True, vmem_limit_bytes=40 << 20
        ),
    )(
        *(
            pltpu.with_memory_space_constraint(x, pltpu.HBM)
            for x in (queries, keys, values, forget, gain.reshape(HEADS, E), grad_out)
        )
    )
    grad_q, grad_k, grad_v, grad_gain = pl.pallas_call(
        store,
        out_shape=shapes,
        in_specs=[vmem] * 4,
        out_specs=(hbm,) * 4,
        scratch_shapes=[pltpu.SemaphoreType.DMA((4,))],
        compiler_params=pltpu.CompilerParams(vmem_limit_bytes=4 << 20),
    )(*grads)
    return grad_q, grad_k, grad_v, grad_gain.reshape(-1)


def solution(mesh):
    in_specs = (
        P("dp", "ctx", "tensor"),
        P("dp", "ctx", "tensor"),
        P("dp", "ctx", "tensor"),
        P("dp", "tensor", "ctx"),
        P("tensor"),
        P("dp", "ctx", "tensor"),
    )
    out_specs = (
        P("dp", "ctx", "tensor"),
        P("dp", "ctx", "tensor"),
        P("dp", "ctx", "tensor"),
        P("tensor"),
    )
    return jax.shard_map(shards, mesh=mesh, in_specs=in_specs, out_specs=out_specs, check_vma=False)
```

```python
import functools

import jax
import jax.numpy as jnp
from jax import lax
from jax.experimental import pallas as pl
from jax.experimental.pallas import tpu as pltpu
from jax.sharding import PartitionSpec as P

E = 128
EPSILON = 1e-05
MESH = pl.DeviceIdType.MESH
F32 = jnp.float32
BF16 = jnp.bfloat16

HEADS = 8
CTX = 64
RING = 8
TENSOR = 4
BATCHES = 2
STAGGER = 2
GROUP = HEADS // BATCHES
OWNERS = CTX // GROUP


def matmul(a, b, contract_a, contract_b):
    return lax.dot_general(
        a, b, (((contract_a,), (contract_b,)), ((), ())), preferred_element_type=F32
    )


def kernel(
    q_hbm, k_hbm, v_hbm, f_hbm, gain_hbm, g_hbm,
    gq_ref, gk_ref, gv_ref, gg_ref,
    q_ref, k_ref, v_ref, f_ref, gain_ref, g_ref,
    state, state_in, prefix, prefix_in,
    back, back_in, suffix, suffix_in,
    decay_out, decay_in,
    weight, weighted, attended, earlier_b, grad_att, part_k, part_v,
    grad_normed, of_query, of_key, query_scaled,
    norm_out, norm_in,
    gain_y_out, gain_y_in, gain_z_out, gain_z_in, gain_dp_out, gain_dp_in,
    decay_sems, state_send, state_recv, prefix_send, prefix_recv,
    back_send, back_recv, suffix_send, suffix_recv,
    norm_sems, gain_y_sems, gain_z_sems, gain_dp_sems, load_sems, turn_sem,
):
    dp, me, tn = lax.axis_index("dp"), lax.axis_index("ctx"), lax.axis_index("tensor")
    z, y = me // RING, lax.rem(me, RING)
    scale = E ** (-0.5)
    full_width = TENSOR * HEADS * E

    def alternate(i):
        half, odd = i // 2, lax.rem(i, 2)
        return half + odd * (RING - 1 - 2 * half)

    def ctx_peer(i):
        i = CTX - i
        to_z, to_y = alternate(i // RING), alternate(lax.rem(i, RING))
        return lax.rem(z + to_z, RING) * RING + lax.rem(y + to_y, RING)

    def tensor_peer(i):
        return lax.rem(tn + i, TENSOR)

    def y_peer(i):
        return z * RING + lax.rem(y + i, RING)

    def z_peer(i):
        return lax.rem(z + i, RING) * RING + y

    loads = [
        pltpu.make_async_copy(source, target, load_sems.at[i])
        for i, (source, target) in enumerate(
            (
                (f_hbm, f_ref), (k_hbm, k_ref), (v_hbm, v_ref),
                (q_hbm, q_ref), (g_hbm, g_ref), (gain_hbm, gain_ref),
            )
        )
    ]
    for load in loads:
        load.start()

    barrier = pltpu.get_barrier_semaphore()

    def greet_ctx(i, carry):
        pl.semaphore_signal(
            barrier, inc=1, device_id=(dp, ctx_peer(i), tn), device_id_type=MESH
        )
        return carry

    def greet_tensor(i, carry):
        pl.semaphore_signal(
            barrier, inc=1, device_id=(dp, me, tensor_peer(i)), device_id_type=MESH
        )
        return carry

    lax.fori_loop(1, CTX, greet_ctx, 0)
    lax.fori_loop(1, TENSOR, greet_tensor, 0)
    pl.semaphore_signal(barrier, inc=1, device_id=(1 - dp, me, tn), device_id_type=MESH)

    def remote(src, dst, send_sem, recv_sem, device):
        return pltpu.make_async_remote_copy(
            src_ref=src, dst_ref=dst, send_sem=send_sem, recv_sem=recv_sem,
            device_id=device, device_id_type=MESH,
        )

    def wait_bytes(ref, sem):
        pltpu.make_async_copy(ref, ref, sem).wait()

    def exchange(src, dst, send_sem, recv_sem):
        def go(i, carry):
            peer = ctx_peer(i)
            remote(src.at[peer], dst.at[me], send_sem, recv_sem, (dp, peer, tn)).start()
            return carry

        lax.fori_loop(1, CTX, go, 0)
        dst[me] = src[me]

    loads[0].wait()
    lanes = lax.broadcasted_iota(jnp.int32, (HEADS, E), 1)
    cumulative = f_ref[0]
    for shift in (1, 2, 4, 8, 16, 32, 64):
        moved = pltpu.roll(cumulative, shift, 1)
        cumulative = cumulative + jnp.where(lanes >= shift, moved, 0.0)
    block_decay = cumulative[:, E - 1 :]
    passing = jnp.broadcast_to(jnp.exp(-block_decay), (HEADS, E))
    for h in range(HEADS):
        decay_out[h % GROUP, h // GROUP] = passing[h]
    cumulative_t = cumulative.T
    query_decay = jnp.exp(-cumulative).T
    key_decay = jnp.exp(-(block_decay - cumulative)).T

    def columns(h):
        return slice(h * E, (h + 1) * E)

    def pieces(h):
        return h // GROUP, slice((h % GROUP) * OWNERS, (h % GROUP + 1) * OWNERS)

    def put_state(ref, h, value):
        batch, rows = pieces(h)
        ref[batch, rows] = value.reshape(OWNERS, 8, E)

    def get_state(ref, h):
        batch, rows = pieces(h)
        return ref[batch, rows].reshape(E, E)

    loads[1].wait()
    loads[2].wait()

    def make_state(h):
        key_scaled = (k_ref[0, :, columns(h)].astype(F32) * key_decay[:, h : h + 1]).astype(BF16)
        put_state(state, h, matmul(key_scaled, v_ref[0, :, columns(h)], 0, 0))

    for h in range(GROUP):
        make_state(h)
    pl.semaphore_wait(barrier, CTX - 1 + TENSOR - 1 + 1)

    def send_decay(i, carry):
        peer = ctx_peer(i)
        remote(
            decay_out.at[peer // OWNERS], decay_in.at[me],
            decay_sems.at[0], decay_sems.at[1], (dp, peer, tn),
        ).start()
        return carry

    @pl.when(dp == 1)
    def _():
        pl.semaphore_wait(turn_sem, 1)

    exchange(state.at[0], state_in.at[0], state_send.at[0], state_recv.at[0])
    lax.fori_loop(1, CTX, send_decay, 0)
    decay_in[me] = decay_out[me // OWNERS]
    for h in range(GROUP, HEADS):
        make_state(h)
    exchange(state.at[1], state_in.at[1], state_send.at[1], state_recv.at[1])
    for load in loads[3:]:
        load.wait()

    below = lax.broadcasted_iota(jnp.int32, (E, E), 0) >= lax.broadcasted_iota(
        jnp.int32, (E, E), 1
    )

    def make_local(h):
        span = cumulative_t[:, h : h + 1] - cumulative[h : h + 1, :]
        now = jnp.where(below, jnp.exp(-jnp.where(below, span, 0.0)), 0.0)
        weight[h] = now
        scores = matmul(q_ref[0, :, columns(h)], k_ref[0, :, columns(h)], 1, 1)
        rounded = (scores * scale * now).astype(BF16)
        weighted[h] = rounded
        attended[h] = matmul(rounded, v_ref[0, :, columns(h)], 1, 0)
        grad_normed[h] = g_ref[0, :, columns(h)].astype(F32) * gain_ref[h : h + 1, :]
        of_query[h] = jnp.broadcast_to(scale * query_decay[:, h : h + 1], (E, E))
        of_key[h] = jnp.broadcast_to(scale * key_decay[:, h : h + 1], (E, E))
        scaled = q_ref[0, :, columns(h)].astype(F32) * query_decay[:, h : h + 1]
        query_scaled[h] = scaled.T.astype(BF16)

    for h in range(GROUP):
        make_local(h)

    others = pl.ds(0, CTX - 1)
    for b in range(STAGGER):
        wait_bytes(state.at[b, others], state_send.at[b])

    @pl.when(dp == 0)
    def _():
        pl.semaphore_signal(turn_sem, inc=1, device_id=(1, me, tn), device_id_type=MESH)

    wait_bytes(decay_in.at[others], decay_sems.at[1])

    def run_scan(b, source, result, reverse):
        def step(i, total):
            at = CTX - 1 - i if reverse else i
            result[b, at] = total
            return total * decay_in[at, b : b + 1] + source[b, at]

        lax.fori_loop(0, CTX, step, jnp.zeros((8, E), F32), unroll=8)

    for b in range(BATCHES):
        wait_bytes(state_in.at[b, others], state_recv.at[b])
        run_scan(b, state_in, prefix, False)
        exchange(prefix.at[b], prefix_in.at[b], prefix_send.at[b], prefix_recv.at[b])
        for h in range(GROUP + 2 * b, GROUP + 2 * b + 2):
            make_local(h)

    squares = jnp.zeros((E, E), F32)
    products = jnp.zeros((E, E), F32)
    for b in range(BATCHES):
        wait_bytes(prefix_in.at[b, others], prefix_recv.at[b])
        for h in range(b * GROUP, (b + 1) * GROUP):
            state_b = get_state(prefix_in, h).astype(BF16)
            earlier_b[h] = state_b
            carried = matmul(q_ref[0, :, columns(h)], state_b, 1, 0)
            now = attended[h] + of_query[h] * carried
            attended[h] = now
            squares = squares + now * now
            products = products + grad_normed[h] * now

    wide = lax.broadcasted_iota(jnp.int32, (E, E), 1)
    both = jnp.where(
        wide == 0,
        jnp.sum(squares, axis=1, keepdims=True),
        jnp.sum(products, axis=1, keepdims=True),
    ).T[0:8]
    norm_out[...] = both

    def send_norm(i, carry):
        remote(
            norm_out, norm_in.at[tn], norm_sems.at[0], norm_sems.at[1], (dp, me, tensor_peer(i))
        ).start()
        return carry

    lax.fori_loop(1, TENSOR, send_norm, 0)
    norm_in[tn] = both
    wait_bytes(norm_in.at[pl.ds(0, TENSOR - 1)], norm_sems.at[1])
    sums = (norm_in[0] + norm_in[1]) + (norm_in[2] + norm_in[3])
    inverse_rms = lax.rsqrt(sums[0:1] / full_width + EPSILON)
    projected = sums[1:2] * inverse_rms / full_width
    of_grad = jnp.broadcast_to(inverse_rms, (E, E)).T
    of_attended = jnp.broadcast_to(inverse_rms * inverse_rms * projected, (E, E)).T

    def make_back(b):
        for h in range(b * GROUP, (b + 1) * GROUP):
            grad_now = (of_grad * grad_normed[h] - of_attended * attended[h]).astype(BF16)
            grad_att[h] = grad_now
            put_state(back, h, matmul(query_scaled[h], grad_now, 1, 0))
        exchange(back.at[b], back_in.at[b], back_send.at[b], back_recv.at[b])

    def sum_ring(out, into, sems, peer_of, mine):
        def go(i, carry):
            remote(out, into.at[mine], sems.at[0], sems.at[1], (dp, peer_of(i), tn)).start()
            return carry

        lax.fori_loop(1, RING, go, 0)
        into[mine] = out[...]

    def ring_total(into, sems):
        wait_bytes(into.at[pl.ds(0, RING - 1)], sems.at[1])
        total = into[0]
        for i in range(1, RING):
            total = total + into[i]
        return total

    make_back(0)
    for h in range(HEADS):
        normed = attended[h] * of_grad
        gain_y_out[h] = jnp.sum(g_ref[0, :, columns(h)].astype(F32) * normed, axis=0)
    sum_ring(gain_y_out, gain_y_in, gain_y_sems, y_peer, y)
    make_back(1)

    def make_parts(h):
        grad_now = grad_att[h]
        scores = matmul(grad_now, v_ref[0, :, columns(h)], 1, 1)
        grad_weighted = (scores * scale * weight[h]).astype(BF16)
        grad_q = matmul(grad_weighted, k_ref[0, :, columns(h)], 1, 0) + of_query[h] * matmul(
            grad_now, earlier_b[h], 1, 1
        )
        gq_ref[0, :, columns(h)] = grad_q.astype(BF16)
        part_k[h] = matmul(grad_weighted, q_ref[0, :, columns(h)], 0, 0)
        part_v[h] = matmul(weighted[h], grad_now, 0, 0)

    for h in range(GROUP):
        make_parts(h)

    gain_z_out[...] = ring_total(gain_y_in, gain_y_sems)
    sum_ring(gain_z_out, gain_z_in, gain_z_sems, z_peer, z)
    other_core = remote(
        gain_dp_out, gain_dp_in, gain_dp_sems.at[0], gain_dp_sems.at[1], (1 - dp, me, tn)
    )
    for b in range(BATCHES):
        wait_bytes(back_in.at[b, others], back_recv.at[b])
        run_scan(b, back_in, suffix, True)
        if b == BATCHES - 1:
            gain_total = ring_total(gain_z_in, gain_z_sems)
            gain_dp_out[...] = gain_total
            other_core.start()
        exchange(suffix.at[b], suffix_in.at[b], suffix_send.at[b], suffix_recv.at[b])
        for h in range(GROUP + 2 * b, GROUP + 2 * b + 2):
            make_parts(h)

    for b in range(BATCHES):
        wait_bytes(suffix_in.at[b, others], suffix_recv.at[b])
        for h in range(b * GROUP, (b + 1) * GROUP):
            later_b = get_state(suffix_in, h).astype(BF16)
            grad_k = part_k[h] + of_key[h] * matmul(v_ref[0, :, columns(h)], later_b, 1, 1)
            grad_v = part_v[h] + of_key[h] * matmul(k_ref[0, :, columns(h)], later_b, 1, 0)
            gk_ref[0, :, columns(h)] = grad_k.astype(BF16)
            gv_ref[0, :, columns(h)] = grad_v.astype(BF16)

    other_core.wait()
    gg_ref[...] = gain_total + gain_dp_in[...]

    wait_bytes(decay_in.at[others], decay_sems.at[0])
    for b in range(STAGGER, BATCHES):
        wait_bytes(state.at[b, others], state_send.at[b])
    for b in range(BATCHES):
        wait_bytes(prefix.at[b, others], prefix_send.at[b])
        wait_bytes(back.at[b, others], back_send.at[b])
        wait_bytes(suffix.at[b, others], suffix_send.at[b])
    wait_bytes(norm_in.at[pl.ds(0, TENSOR - 1)], norm_sems.at[0])
    wait_bytes(gain_y_in.at[pl.ds(0, RING - 1)], gain_y_sems.at[0])
    wait_bytes(gain_z_in.at[pl.ds(0, RING - 1)], gain_z_sems.at[0])


def store(*refs):
    sources, targets, sems = refs[:4], refs[4:8], refs[8]
    copies = [
        pltpu.make_async_copy(source, target, sems.at[i])
        for i, (source, target) in enumerate(zip(sources, targets))
    ]
    for copy in copies:
        copy.start()
    for copy in copies:
        copy.wait()


def shards(queries, keys, values, forget, gain, grad_out):
    block = jax.ShapeDtypeStruct(queries.shape, BF16)
    states = pltpu.VMEM((BATCHES, CTX, 8, E), F32)
    squares_f32 = pltpu.VMEM((HEADS, E, E), F32)
    squares_bf16 = pltpu.VMEM((HEADS, E, E), BF16)
    tile = pltpu.VMEM((8, E), F32)
    ring = pltpu.VMEM((RING, 8, E), F32)
    pair = pltpu.SemaphoreType.DMA((2,))
    vmem = pl.BlockSpec(memory_space=pltpu.VMEM)
    hbm = pl.BlockSpec(memory_space=pltpu.HBM)
    tokens = pltpu.VMEM(queries.shape, BF16)
    shapes = (block, block, block, jax.ShapeDtypeStruct((HEADS, E), F32))
    grads = pl.pallas_call(
        kernel,
        out_shape=shapes,
        in_specs=[hbm] * 6,
        out_specs=(vmem,) * 4,
        scratch_shapes=[tokens, tokens, tokens, pltpu.VMEM(forget.shape, F32), tile, tokens]
        + [states] * 8
        + [pltpu.VMEM((GROUP, BATCHES, E), F32), pltpu.VMEM((CTX, BATCHES, E), F32)]
        + [squares_f32, squares_bf16, squares_f32, squares_bf16, squares_bf16]
        + [squares_f32] * 5
        + [squares_bf16]
        + [tile, pltpu.VMEM((TENSOR, 8, E), F32)]
        + [tile, ring, tile, ring, tile, tile]
        + [pair] * 13
        + [pltpu.SemaphoreType.DMA((6,)), pltpu.SemaphoreType.REGULAR],
        compiler_params=pltpu.CompilerParams(
            collective_id=0, has_side_effects=True, vmem_limit_bytes=40 << 20
        ),
    )(
        *(
            pltpu.with_memory_space_constraint(x, pltpu.HBM)
            for x in (queries, keys, values, forget, gain.reshape(HEADS, E), grad_out)
        )
    )
    grad_q, grad_k, grad_v, grad_gain = pl.pallas_call(
        store,
        out_shape=shapes,
        in_specs=[vmem] * 4,
        out_specs=(hbm,) * 4,
        scratch_shapes=[pltpu.SemaphoreType.DMA((4,))],
        compiler_params=pltpu.CompilerParams(vmem_limit_bytes=4 << 20),
    )(*grads)
    return grad_q, grad_k, grad_v, grad_gain.reshape(-1)


def solution(mesh):
    in_specs = (
        P("dp", "ctx", "tensor"),
        P("dp", "ctx", "tensor"),
        P("dp", "ctx", "tensor"),
        P("dp", "tensor", "ctx"),
        P("tensor"),
        P("dp", "ctx", "tensor"),
    )
    out_specs = (
        P("dp", "ctx", "tensor"),
        P("dp", "ctx", "tensor"),
        P("dp", "ctx", "tensor"),
        P("tensor"),
    )
    return jax.shard_map(shards, mesh=mesh, in_specs=in_specs, out_specs=out_specs, check_vma=False)
```

```python
import functools

import jax
import jax.numpy as jnp
from jax import lax
from jax.experimental import pallas as pl
from jax.experimental.pallas import tpu as pltpu
from jax.sharding import PartitionSpec as P

E = 128
EPSILON = 1e-05
MESH = pl.DeviceIdType.MESH
F32 = jnp.float32
BF16 = jnp.bfloat16

HEADS = 8
RING = 8
TENSOR = 4
BATCHES = 4
GROUP = HEADS // BATCHES
SPLIT = RING // GROUP
ROWS = E // SPLIT
FULL = pl.ds(0, ROWS + 1)


def matmul(a, b, contract_a, contract_b):
    return lax.dot_general(
        a, b, (((contract_a,), (contract_b,)), ((), ())), preferred_element_type=F32
    )


def kernel(
    q_hbm, k_hbm, v_hbm, f_hbm, gain_hbm, g_hbm,
    gq_ref, gk_ref, gv_ref, gg_ref,
    q_ref, k_ref, v_ref, f_ref, gain_ref, g_ref,
    state, state_in, row_out, row_in, prefix, prefix_in,
    back, back_in, row_back_out, row_back_in, suffix, suffix_in,
    weight, weighted, attended, earlier_b, grad_att, part_k, part_v,
    grad_normed, of_query, of_key, query_scaled,
    norm_out, norm_in,
    gain_y_out, gain_y_in, gain_z_out, gain_z_in, gain_dp_out, gain_dp_in,
    state_send, state_recv, row_send, row_recv, prefix_send, prefix_recv,
    back_send, back_recv, row_back_send, row_back_recv, suffix_send, suffix_recv,
    norm_sems, gain_y_sems, gain_z_sems, gain_dp_sems, load_sems,
):
    dp, me, tn = lax.axis_index("dp"), lax.axis_index("ctx"), lax.axis_index("tensor")
    z, y = me // RING, lax.rem(me, RING)
    scale = E ** (-0.5)
    full_width = TENSOR * HEADS * E

    def tensor_peer(i):
        return lax.rem(tn + i, TENSOR)

    def y_peer(i):
        return z * RING + lax.rem(y + i, RING)

    def z_peer(i):
        return lax.rem(z + i, RING) * RING + y

    loads = [
        pltpu.make_async_copy(source, target, load_sems.at[i])
        for i, (source, target) in enumerate(
            (
                (f_hbm, f_ref), (k_hbm, k_ref), (v_hbm, v_ref),
                (q_hbm, q_ref), (g_hbm, g_ref), (gain_hbm, gain_ref),
            )
        )
    ]
    for load in loads:
        load.start()

    barrier = pltpu.get_barrier_semaphore()

    for i in range(1, RING):
        for peer in (y_peer(i), z_peer(i)):
            pl.semaphore_signal(barrier, inc=1, device_id=(dp, peer, tn), device_id_type=MESH)
    for i in range(1, TENSOR):
        pl.semaphore_signal(
            barrier, inc=1, device_id=(dp, me, tensor_peer(i)), device_id_type=MESH
        )
    pl.semaphore_signal(barrier, inc=1, device_id=(1 - dp, me, tn), device_id_type=MESH)
    greeted = 2 * (RING - 1) + TENSOR - 1 + 1

    def remote(src, dst, send_sem, recv_sem, device):
        return pltpu.make_async_remote_copy(
            src_ref=src, dst_ref=dst, send_sem=send_sem, recv_sem=recv_sem,
            device_id=device, device_id_type=MESH,
        )

    def wait_bytes(ref, sem):
        pltpu.make_async_copy(ref, ref, sem).wait()

    others = pl.ds(0, RING - 1)
    far_first = (4, 3, 5, 2, 6, 1, 7)

    def exchange(src, dst, send_sem, recv_sem, rows):
        for i in far_first:
            peer = lax.rem(y + i, RING)
            remote(
                src.at[peer, rows], dst.at[y, rows], send_sem, recv_sem,
                (dp, z * RING + peer, tn),
            ).start()
        dst[y, rows] = src[y, rows]

    def row_peers(later):
        for i in range(RING - 1, 0, -1):
            peer = z + i if later else z - i
            yield i, peer, (peer < RING) if later else (peer >= 0)

    def send_row(out, into, send_sems, recv_sems, later):
        for i, peer, exists in row_peers(later):

            @pl.when(exists)
            def _(i=i, peer=peer):
                remote(
                    out.at[FULL], into.at[z, FULL], send_sems.at[i], recv_sems.at[z],
                    (dp, peer * RING + y, tn),
                ).start()

    def row_sent(out, send_sems, later):
        for i, _, exists in row_peers(later):

            @pl.when(exists)
            def _(i=i):
                wait_bytes(out.at[FULL], send_sems.at[i])

    def row_arrived(into, recv_sems, later):
        for i, peer, exists in row_peers(not later):

            @pl.when(exists)
            def _(peer=peer):
                wait_bytes(into.at[peer, FULL], recv_sems.at[peer])

    def row_total(source, out, reverse):
        total = jnp.zeros((ROWS, E), F32)
        decay = jnp.ones((1, E), F32)
        for at in range(RING - 1, -1, -1) if reverse else range(RING):
            passing = source[at, ROWS : ROWS + 1]
            total = total * passing + source[at, 0:ROWS]
            decay = decay * passing
        out[0:ROWS] = total
        out[ROWS : ROWS + 1] = decay

    def run_scan(source, rows, result, reverse):
        def of_row(i, total):
            at = RING - 1 - i if reverse else i
            return total * rows[at, ROWS : ROWS + 1] + rows[at, 0:ROWS]

        total = lax.fori_loop(
            0, RING - 1 - z if reverse else z, of_row, jnp.zeros((ROWS, E), F32)
        )
        for at in range(RING - 1, -1, -1) if reverse else range(RING):
            result[at] = total
            total = total * source[at, ROWS : ROWS + 1] + source[at, 0:ROWS]

    loads[0].wait()
    lanes = lax.broadcasted_iota(jnp.int32, (HEADS, E), 1)
    cumulative = f_ref[0]
    for shift in (1, 2, 4, 8, 16, 32, 64):
        moved = pltpu.roll(cumulative, shift, 1)
        cumulative = cumulative + jnp.where(lanes >= shift, moved, 0.0)
    block_decay = cumulative[:, E - 1 :]
    passing = jnp.broadcast_to(jnp.exp(-block_decay), (HEADS, E))
    cumulative_t = cumulative.T
    query_decay = jnp.exp(-cumulative).T
    key_decay = jnp.exp(-(block_decay - cumulative)).T

    def columns(h):
        return slice(h * E, (h + 1) * E)

    def pieces(h):
        return h // GROUP, slice((h % GROUP) * SPLIT, (h % GROUP + 1) * SPLIT)

    def put_state(ref, h, value):
        batch, owners = pieces(h)
        ref[batch, owners, 0:ROWS] = value.reshape(SPLIT, ROWS, E)
        ref[batch, owners, ROWS : ROWS + 1] = jnp.broadcast_to(passing[h], (SPLIT, 1, E))

    def get_state(ref, h):
        batch, owners = pieces(h)
        return ref[batch, owners].reshape(E, E)

    loads[1].wait()
    loads[2].wait()

    def make_state(h):
        key_scaled = (k_ref[0, :, columns(h)].astype(F32) * key_decay[:, h : h + 1]).astype(BF16)
        put_state(state, h, matmul(key_scaled, v_ref[0, :, columns(h)], 0, 0))

    for h in range(HEADS):
        make_state(h)
    pl.semaphore_wait(barrier, greeted)
    for b in range(BATCHES):
        exchange(state.at[b], state_in.at[b], state_send.at[b], state_recv.at[b], FULL)
    for load in loads[3:]:
        load.wait()

    below = lax.broadcasted_iota(jnp.int32, (E, E), 0) >= lax.broadcasted_iota(
        jnp.int32, (E, E), 1
    )

    def make_local(h):
        span = cumulative_t[:, h : h + 1] - cumulative[h : h + 1, :]
        now = jnp.where(below, jnp.exp(-jnp.where(below, span, 0.0)), 0.0)
        weight[h] = now
        scores = matmul(q_ref[0, :, columns(h)], k_ref[0, :, columns(h)], 1, 1)
        rounded = (scores * scale * now).astype(BF16)
        weighted[h] = rounded
        attended[h] = matmul(rounded, v_ref[0, :, columns(h)], 1, 0)
        grad_normed[h] = g_ref[0, :, columns(h)].astype(F32) * gain_ref[h : h + 1, :]
        of_query[h] = jnp.broadcast_to(scale * query_decay[:, h : h + 1], (E, E))
        of_key[h] = jnp.broadcast_to(scale * key_decay[:, h : h + 1], (E, E))
        scaled = q_ref[0, :, columns(h)].astype(F32) * query_decay[:, h : h + 1]
        query_scaled[h] = scaled.T.astype(BF16)

    for h in range(HEADS):
        make_local(h)
    for b in range(BATCHES):
        wait_bytes(state_in.at[b, others, FULL], state_recv.at[b])
        row_total(state_in.at[b], row_out.at[b], False)
        send_row(row_out.at[b], row_in.at[b], row_send.at[b], row_recv.at[b], True)
    for b in range(BATCHES):
        row_arrived(row_in.at[b], row_recv.at[b], True)
        run_scan(state_in.at[b], row_in.at[b], prefix.at[b], False)
        exchange(
            prefix.at[b], prefix_in.at[b], prefix_send.at[b], prefix_recv.at[b], pl.ds(0, ROWS)
        )

    squares = jnp.zeros((E, E), F32)
    products = jnp.zeros((E, E), F32)
    for b in range(BATCHES):
        wait_bytes(prefix_in.at[b, others], prefix_recv.at[b])
        for h in range(b * GROUP, (b + 1) * GROUP):
            state_b = get_state(prefix_in, h).astype(BF16)
            earlier_b[h] = state_b
            carried = matmul(q_ref[0, :, columns(h)], state_b, 1, 0)
            now = attended[h] + of_query[h] * carried
            attended[h] = now
            squares = squares + now * now
            products = products + grad_normed[h] * now

    wide = lax.broadcasted_iota(jnp.int32, (E, E), 1)
    both = jnp.where(
        wide == 0,
        jnp.sum(squares, axis=1, keepdims=True),
        jnp.sum(products, axis=1, keepdims=True),
    ).T[0:8]
    norm_out[...] = both

    def send_norm(i, carry):
        remote(
            norm_out, norm_in.at[tn], norm_sems.at[0], norm_sems.at[1], (dp, me, tensor_peer(i))
        ).start()
        return carry

    lax.fori_loop(1, TENSOR, send_norm, 0)
    norm_in[tn] = both
    wait_bytes(norm_in.at[pl.ds(0, TENSOR - 1)], norm_sems.at[1])
    sums = (norm_in[0] + norm_in[1]) + (norm_in[2] + norm_in[3])
    inverse_rms = lax.rsqrt(sums[0:1] / full_width + EPSILON)
    projected = sums[1:2] * inverse_rms / full_width
    of_grad = jnp.broadcast_to(inverse_rms, (E, E)).T
    of_attended = jnp.broadcast_to(inverse_rms * inverse_rms * projected, (E, E)).T

    def make_back(b):
        for h in range(b * GROUP, (b + 1) * GROUP):
            grad_now = (of_grad * grad_normed[h] - of_attended * attended[h]).astype(BF16)
            grad_att[h] = grad_now
            put_state(back, h, matmul(query_scaled[h], grad_now, 1, 0))
        exchange(back.at[b], back_in.at[b], back_send.at[b], back_recv.at[b], FULL)

    def sum_ring(out, into, sems, peer_of, mine):
        def go(i, carry):
            remote(out, into.at[mine], sems.at[0], sems.at[1], (dp, peer_of(i), tn)).start()
            return carry

        lax.fori_loop(1, RING, go, 0)
        into[mine] = out[...]

    def ring_total(into, sems):
        wait_bytes(into.at[pl.ds(0, RING - 1)], sems.at[1])
        total = into[0]
        for i in range(1, RING):
            total = total + into[i]
        return total

    for b in range(BATCHES):
        make_back(b)
    for h in range(HEADS):
        normed = attended[h] * of_grad
        gain_y_out[h] = jnp.sum(g_ref[0, :, columns(h)].astype(F32) * normed, axis=0)
    sum_ring(gain_y_out, gain_y_in, gain_y_sems, y_peer, y)

    def make_parts(h):
        grad_now = grad_att[h]
        scores = matmul(grad_now, v_ref[0, :, columns(h)], 1, 1)
        grad_weighted = (scores * scale * weight[h]).astype(BF16)
        grad_q = matmul(grad_weighted, k_ref[0, :, columns(h)], 1, 0) + of_query[h] * matmul(
            grad_now, earlier_b[h], 1, 1
        )
        gq_ref[0, :, columns(h)] = grad_q.astype(BF16)
        part_k[h] = matmul(grad_weighted, q_ref[0, :, columns(h)], 0, 0)
        part_v[h] = matmul(weighted[h], grad_now, 0, 0)

    for h in range(HEADS):
        make_parts(h)
    for b in range(BATCHES):
        wait_bytes(back_in.at[b, others, FULL], back_recv.at[b])
        row_total(back_in.at[b], row_back_out.at[b], True)
        send_row(
            row_back_out.at[b], row_back_in.at[b], row_back_send.at[b], row_back_recv.at[b], False
        )
    gain_z_out[...] = ring_total(gain_y_in, gain_y_sems)
    sum_ring(gain_z_out, gain_z_in, gain_z_sems, z_peer, z)
    for b in range(BATCHES):
        row_arrived(row_back_in.at[b], row_back_recv.at[b], False)
        run_scan(back_in.at[b], row_back_in.at[b], suffix.at[b], True)
        exchange(
            suffix.at[b], suffix_in.at[b], suffix_send.at[b], suffix_recv.at[b], pl.ds(0, ROWS)
        )
    gain_total = ring_total(gain_z_in, gain_z_sems)
    gain_dp_out[...] = gain_total
    other_core = remote(
        gain_dp_out, gain_dp_in, gain_dp_sems.at[0], gain_dp_sems.at[1], (1 - dp, me, tn)
    )
    other_core.start()
    for b in range(BATCHES):
        wait_bytes(suffix_in.at[b, others], suffix_recv.at[b])
        for h in range(b * GROUP, (b + 1) * GROUP):
            later_b = get_state(suffix_in, h).astype(BF16)
            grad_k = part_k[h] + of_key[h] * matmul(v_ref[0, :, columns(h)], later_b, 1, 1)
            grad_v = part_v[h] + of_key[h] * matmul(k_ref[0, :, columns(h)], later_b, 1, 0)
            gk_ref[0, :, columns(h)] = grad_k.astype(BF16)
            gv_ref[0, :, columns(h)] = grad_v.astype(BF16)

    other_core.wait()
    gg_ref[...] = gain_total + gain_dp_in[...]

    for b in range(BATCHES):
        wait_bytes(state.at[b, others, FULL], state_send.at[b])
        row_sent(row_out.at[b], row_send.at[b], True)
        wait_bytes(prefix.at[b, others], prefix_send.at[b])
        wait_bytes(back.at[b, others, FULL], back_send.at[b])
        row_sent(row_back_out.at[b], row_back_send.at[b], False)
        wait_bytes(suffix.at[b, others], suffix_send.at[b])
    wait_bytes(norm_in.at[pl.ds(0, TENSOR - 1)], norm_sems.at[0])
    wait_bytes(gain_y_in.at[pl.ds(0, RING - 1)], gain_y_sems.at[0])
    wait_bytes(gain_z_in.at[pl.ds(0, RING - 1)], gain_z_sems.at[0])


def store(*refs):
    sources, targets, sems = refs[:4], refs[4:8], refs[8]
    copies = [
        pltpu.make_async_copy(source, target, sems.at[i])
        for i, (source, target) in enumerate(zip(sources, targets))
    ]
    for copy in copies:
        copy.start()
    for copy in copies:
        copy.wait()


def shards(queries, keys, values, forget, gain, grad_out):
    block = jax.ShapeDtypeStruct(queries.shape, BF16)
    rows = pltpu.VMEM((BATCHES, RING, ROWS, E), F32)
    rows_more = pltpu.VMEM((BATCHES, RING, ROWS + 8, E), F32)
    total = pltpu.VMEM((BATCHES, ROWS + 8, E), F32)
    one_scan = [rows_more, rows_more, total, rows_more, rows, rows]
    squares_f32 = pltpu.VMEM((HEADS, E, E), F32)
    squares_bf16 = pltpu.VMEM((HEADS, E, E), BF16)
    tile = pltpu.VMEM((8, E), F32)
    ring = pltpu.VMEM((RING, 8, E), F32)
    pair = pltpu.SemaphoreType.DMA((2,))
    each = pltpu.SemaphoreType.DMA((BATCHES,))
    each_row = pltpu.SemaphoreType.DMA((BATCHES, RING))
    scan_sems = [each, each, each_row, each_row, each, each]
    vmem = pl.BlockSpec(memory_space=pltpu.VMEM)
    hbm = pl.BlockSpec(memory_space=pltpu.HBM)
    tokens = pltpu.VMEM(queries.shape, BF16)
    shapes = (block, block, block, jax.ShapeDtypeStruct((HEADS, E), F32))
    grads = pl.pallas_call(
        kernel,
        out_shape=shapes,
        in_specs=[hbm] * 6,
        out_specs=(vmem,) * 4,
        scratch_shapes=[tokens, tokens, tokens, pltpu.VMEM(forget.shape, F32), tile, tokens]
        + one_scan * 2
        + [squares_f32, squares_bf16, squares_f32, squares_bf16, squares_bf16]
        + [squares_f32] * 5
        + [squares_bf16]
        + [tile, pltpu.VMEM((TENSOR, 8, E), F32)]
        + [tile, ring, tile, ring, tile, tile]
        + scan_sems * 2
        + [pair] * 4
        + [pltpu.SemaphoreType.DMA((6,))],
        compiler_params=pltpu.CompilerParams(
            collective_id=0, has_side_effects=True, vmem_limit_bytes=40 << 20
        ),
    )(
        *(
            pltpu.with_memory_space_constraint(x, pltpu.HBM)
            for x in (queries, keys, values, forget, gain.reshape(HEADS, E), grad_out)
        )
    )
    grad_q, grad_k, grad_v, grad_gain = pl.pallas_call(
        store,
        out_shape=shapes,
        in_specs=[vmem] * 4,
        out_specs=(hbm,) * 4,
        scratch_shapes=[pltpu.SemaphoreType.DMA((4,))],
        compiler_params=pltpu.CompilerParams(vmem_limit_bytes=4 << 20),
    )(*grads)
    return grad_q, grad_k, grad_v, grad_gain.reshape(-1)


def solution(mesh):
    in_specs = (
        P("dp", "ctx", "tensor"),
        P("dp", "ctx", "tensor"),
        P("dp", "ctx", "tensor"),
        P("dp", "tensor", "ctx"),
        P("tensor"),
        P("dp", "ctx", "tensor"),
    )
    out_specs = (
        P("dp", "ctx", "tensor"),
        P("dp", "ctx", "tensor"),
        P("dp", "ctx", "tensor"),
        P("tensor"),
    )
    return jax.shard_map(shards, mesh=mesh, in_specs=in_specs, out_specs=out_specs, check_vma=False)
```

```python
import functools

import jax
import jax.numpy as jnp
from jax import lax
from jax.experimental import pallas as pl
from jax.experimental.pallas import tpu as pltpu
from jax.sharding import PartitionSpec as P

E = 128
EPSILON = 1e-05
MESH = pl.DeviceIdType.MESH
F32 = jnp.float32
BF16 = jnp.bfloat16

HEADS = 8
RING = 8
FAR_FIRST = (4, 3, 5, 2, 6, 1, 7)
TENSOR = 4
BATCHES = 4
GROUP = HEADS // BATCHES
SPLIT = RING // GROUP
ROWS = E // SPLIT
PART = pl.ds(0, ROWS)
FULL = pl.ds(0, ROWS + 1)


def matmul(a, b, contract_a, contract_b):
    return lax.dot_general(
        a, b, (((contract_a,), (contract_b,)), ((), ())), preferred_element_type=F32
    )


def kernel(
    q_hbm, k_hbm, v_hbm, f_hbm, gain_hbm, g_hbm,
    gq_ref, gk_ref, gv_ref, gg_ref,
    q_ref, k_ref, v_ref, f_ref, gain_ref, g_ref,
    state, state_in, row_out, row_in, prefix, prefix_in,
    back, back_in, row_back_out, row_back_in, suffix, suffix_in,
    weight, weighted, attended, earlier_b, grad_att, part_k, part_v,
    grad_normed, of_query, of_key, query_scaled,
    norm_out, norm_in,
    gain_y_out, gain_y_in, gain_z_out, gain_z_in, gain_dp_out, gain_dp_in,
    state_send, state_recv, row_send, row_recv, prefix_send, prefix_recv,
    back_send, back_recv, row_back_send, row_back_recv, suffix_send, suffix_recv,
    norm_sems, gain_y_sems, gain_z_sems, gain_dp_sems, load_sems,
):
    dp, me, tn = lax.axis_index("dp"), lax.axis_index("ctx"), lax.axis_index("tensor")
    z, y = me // RING, lax.rem(me, RING)
    scale = E ** (-0.5)
    full_width = TENSOR * HEADS * E

    def tensor_peer(i):
        return lax.rem(tn + i, TENSOR)

    def y_peer(i):
        return z * RING + lax.rem(y + i, RING)

    def z_peer(i):
        return lax.rem(z + i, RING) * RING + y

    barrier = pltpu.get_barrier_semaphore()

    for i in FAR_FIRST:
        for peer in (y_peer(i), z_peer(i)):
            pl.semaphore_signal(barrier, inc=1, device_id=(dp, peer, tn), device_id_type=MESH)
    for i in range(1, TENSOR):
        pl.semaphore_signal(
            barrier, inc=1, device_id=(dp, me, tensor_peer(i)), device_id_type=MESH
        )
    pl.semaphore_signal(barrier, inc=1, device_id=(1 - dp, me, tn), device_id_type=MESH)
    greeted = 2 * (RING - 1) + TENSOR - 1 + 1

    loads = [
        pltpu.make_async_copy(source, target, load_sems.at[i])
        for i, (source, target) in enumerate(
            (
                (f_hbm, f_ref), (k_hbm, k_ref), (v_hbm, v_ref),
                (q_hbm, q_ref), (g_hbm, g_ref), (gain_hbm, gain_ref),
            )
        )
    ]
    for load in loads:
        load.start()

    def remote(src, dst, send_sem, recv_sem, device):
        return pltpu.make_async_remote_copy(
            src_ref=src, dst_ref=dst, send_sem=send_sem, recv_sem=recv_sem,
            device_id=device, device_id_type=MESH,
        )

    def wait_bytes(ref, sem):
        pltpu.make_async_copy(ref, ref, sem).wait()

    others = pl.ds(0, RING - 1)

    def exchange(src, dst, send_sem, recv_sem, rows):
        for i in FAR_FIRST:
            peer = lax.rem(y + jnp.where(dp == 0, i, RING - i), RING)
            remote(
                src.at[peer, rows], dst.at[y, rows], send_sem, recv_sem,
                (dp, z * RING + peer, tn),
            ).start()
        dst[y, rows] = src[y, rows]

    def row_peers(later):
        for i in FAR_FIRST:
            peer = z + i if later else z - i
            yield i, peer, (peer < RING) if later else (peer >= 0)

    def send_row(out, into, send_sems, recv_sems, later):
        for i, peer, exists in row_peers(later):

            @pl.when(exists)
            def _(i=i, peer=peer):
                remote(
                    out.at[FULL], into.at[z, FULL], send_sems.at[i], recv_sems.at[z],
                    (dp, peer * RING + y, tn),
                ).start()

    def row_sent(out, send_sems, later):
        for i, _, exists in row_peers(later):

            @pl.when(exists)
            def _(i=i):
                wait_bytes(out.at[FULL], send_sems.at[i])

    def row_arrived(into, recv_sems, later):
        for i, peer, exists in row_peers(not later):

            @pl.when(exists)
            def _(peer=peer):
                wait_bytes(into.at[peer, FULL], recv_sems.at[peer])

    def row_total(source, decays, out, reverse):
        total = jnp.zeros((ROWS, E), F32)
        decay = jnp.ones((1, E), F32)
        for at in range(RING - 1, -1, -1) if reverse else range(RING):
            passed = decays[at, ROWS : ROWS + 1]
            total = total * passed + source[at]
            decay = decay * passed
        out[0:ROWS] = total
        out[ROWS : ROWS + 1] = decay

    def run_scan(source, decays, rows, result, reverse):
        def of_row(i, total):
            at = RING - 1 - i if reverse else i
            return total * rows[at, ROWS : ROWS + 1] + rows[at, 0:ROWS]

        total = lax.fori_loop(
            0, RING - 1 - z if reverse else z, of_row, jnp.zeros((ROWS, E), F32)
        )
        for at in range(RING - 1, -1, -1) if reverse else range(RING):
            result[at] = total
            total = total * decays[at, ROWS : ROWS + 1] + source[at]

    loads[0].wait()
    lanes = lax.broadcasted_iota(jnp.int32, (HEADS, E), 1)
    cumulative = f_ref[0]
    for shift in (1, 2, 4, 8, 16, 32, 64):
        moved = pltpu.roll(cumulative, shift, 1)
        cumulative = cumulative + jnp.where(lanes >= shift, moved, 0.0)
    block_decay = cumulative[:, E - 1 :]
    passing = jnp.broadcast_to(jnp.exp(-block_decay), (HEADS, E))
    cumulative_t = cumulative.T
    query_decay = jnp.exp(-cumulative).T
    key_decay = jnp.exp(-(block_decay - cumulative)).T

    def columns(h):
        return slice(h * E, (h + 1) * E)

    def pieces(h):
        return h // GROUP, slice((h % GROUP) * SPLIT, (h % GROUP + 1) * SPLIT)

    def put_state(ref, h, value):
        batch, owners = pieces(h)
        ref[batch, owners, 0:ROWS] = value.reshape(SPLIT, ROWS, E)

    def get_state(ref, h):
        batch, owners = pieces(h)
        return ref[batch, owners].reshape(E, E)

    loads[1].wait()
    loads[2].wait()

    def make_state(h):
        key_scaled = (k_ref[0, :, columns(h)].astype(F32) * key_decay[:, h : h + 1]).astype(BF16)
        put_state(state, h, matmul(key_scaled, v_ref[0, :, columns(h)], 0, 0))
        batch, owners = pieces(h)
        state[batch, owners, ROWS : ROWS + 1] = jnp.broadcast_to(passing[h], (SPLIT, 1, E))

    for h in range(HEADS):
        make_state(h)
    pl.semaphore_wait(barrier, greeted)
    for b in range(BATCHES):
        exchange(state.at[b], state_in.at[b], state_send.at[b], state_recv.at[b], FULL)
    for load in loads[3:]:
        load.wait()

    below = lax.broadcasted_iota(jnp.int32, (E, E), 0) >= lax.broadcasted_iota(
        jnp.int32, (E, E), 1
    )

    def make_local(h):
        span = cumulative_t[:, h : h + 1] - cumulative[h : h + 1, :]
        now = jnp.where(below, jnp.exp(-jnp.where(below, span, 0.0)), 0.0)
        weight[h] = now
        scores = matmul(q_ref[0, :, columns(h)], k_ref[0, :, columns(h)], 1, 1)
        rounded = (scores * scale * now).astype(BF16)
        weighted[h] = rounded
        attended[h] = matmul(rounded, v_ref[0, :, columns(h)], 1, 0)
        grad_normed[h] = g_ref[0, :, columns(h)].astype(F32) * gain_ref[h : h + 1, :]
        of_query[h] = jnp.broadcast_to(scale * query_decay[:, h : h + 1], (E, E))
        of_key[h] = jnp.broadcast_to(scale * key_decay[:, h : h + 1], (E, E))
        scaled = q_ref[0, :, columns(h)].astype(F32) * query_decay[:, h : h + 1]
        query_scaled[h] = scaled.T.astype(BF16)

    for h in range(HEADS):
        make_local(h)
    for b in range(BATCHES):
        wait_bytes(state_in.at[b, others, FULL], state_recv.at[b])
        row_total(state_in.at[b, :, 0:ROWS], state_in.at[b], row_out.at[b], False)
        send_row(row_out.at[b], row_in.at[b], row_send.at[b], row_recv.at[b], True)
    for b in range(BATCHES):
        row_arrived(row_in.at[b], row_recv.at[b], True)
        run_scan(state_in.at[b, :, 0:ROWS], state_in.at[b], row_in.at[b], prefix.at[b], False)
        exchange(
            prefix.at[b], prefix_in.at[b], prefix_send.at[b], prefix_recv.at[b], PART
        )

    squares = jnp.zeros((E, E), F32)
    products = jnp.zeros((E, E), F32)
    for b in range(BATCHES):
        wait_bytes(prefix_in.at[b, others], prefix_recv.at[b])
        for h in range(b * GROUP, (b + 1) * GROUP):
            state_b = get_state(prefix_in, h).astype(BF16)
            earlier_b[h] = state_b
            carried = matmul(q_ref[0, :, columns(h)], state_b, 1, 0)
            now = attended[h] + of_query[h] * carried
            attended[h] = now
            squares = squares + now * now
            products = products + grad_normed[h] * now

    wide = lax.broadcasted_iota(jnp.int32, (E, E), 1)
    both = jnp.where(
        wide == 0,
        jnp.sum(squares, axis=1, keepdims=True),
        jnp.sum(products, axis=1, keepdims=True),
    ).T[0:8]
    norm_out[...] = both

    def send_norm(i, carry):
        remote(
            norm_out, norm_in.at[tn], norm_sems.at[0], norm_sems.at[1], (dp, me, tensor_peer(i))
        ).start()
        return carry

    lax.fori_loop(1, TENSOR, send_norm, 0)
    norm_in[tn] = both
    wait_bytes(norm_in.at[pl.ds(0, TENSOR - 1)], norm_sems.at[1])
    sums = (norm_in[0] + norm_in[1]) + (norm_in[2] + norm_in[3])
    inverse_rms = lax.rsqrt(sums[0:1] / full_width + EPSILON)
    projected = sums[1:2] * inverse_rms / full_width
    of_grad = jnp.broadcast_to(inverse_rms, (E, E)).T
    of_attended = jnp.broadcast_to(inverse_rms * inverse_rms * projected, (E, E)).T

    def make_back(b):
        for h in range(b * GROUP, (b + 1) * GROUP):
            grad_now = (of_grad * grad_normed[h] - of_attended * attended[h]).astype(BF16)
            grad_att[h] = grad_now
            put_state(back, h, matmul(query_scaled[h], grad_now, 1, 0))
        exchange(back.at[b], back_in.at[b], back_send.at[b], back_recv.at[b], PART)

    def sum_ring(out, into, sems, peer_of, mine):
        def go(i, carry):
            remote(out, into.at[mine], sems.at[0], sems.at[1], (dp, peer_of(i), tn)).start()
            return carry

        lax.fori_loop(1, RING, go, 0)
        into[mine] = out[...]

    def ring_total(into, sems):
        wait_bytes(into.at[pl.ds(0, RING - 1)], sems.at[1])
        total = into[0]
        for i in range(1, RING):
            total = total + into[i]
        return total

    for b in range(BATCHES):
        make_back(b)
    for h in range(HEADS):
        normed = attended[h] * of_grad
        gain_y_out[h] = jnp.sum(g_ref[0, :, columns(h)].astype(F32) * normed, axis=0)
    sum_ring(gain_y_out, gain_y_in, gain_y_sems, y_peer, y)

    def make_parts(h):
        grad_now = grad_att[h]
        scores = matmul(grad_now, v_ref[0, :, columns(h)], 1, 1)
        grad_weighted = (scores * scale * weight[h]).astype(BF16)
        grad_q = matmul(grad_weighted, k_ref[0, :, columns(h)], 1, 0) + of_query[h] * matmul(
            grad_now, earlier_b[h], 1, 1
        )
        gq_ref[0, :, columns(h)] = grad_q.astype(BF16)
        part_k[h] = matmul(grad_weighted, q_ref[0, :, columns(h)], 0, 0)
        part_v[h] = matmul(weighted[h], grad_now, 0, 0)

    for h in range(HEADS):
        make_parts(h)
    for b in range(BATCHES):
        wait_bytes(back_in.at[b, others], back_recv.at[b])
        row_total(back_in.at[b], state_in.at[b], row_back_out.at[b], True)
        send_row(
            row_back_out.at[b], row_back_in.at[b], row_back_send.at[b], row_back_recv.at[b], False
        )
    gain_z_out[...] = ring_total(gain_y_in, gain_y_sems)
    sum_ring(gain_z_out, gain_z_in, gain_z_sems, z_peer, z)
    for b in range(BATCHES):
        row_arrived(row_back_in.at[b], row_back_recv.at[b], False)
        run_scan(back_in.at[b], state_in.at[b], row_back_in.at[b], suffix.at[b], True)
        exchange(
            suffix.at[b], suffix_in.at[b], suffix_send.at[b], suffix_recv.at[b], PART
        )
    gain_total = ring_total(gain_z_in, gain_z_sems)
    gain_dp_out[...] = gain_total
    other_core = remote(
        gain_dp_out, gain_dp_in, gain_dp_sems.at[0], gain_dp_sems.at[1], (1 - dp, me, tn)
    )
    other_core.start()
    for b in range(BATCHES):
        wait_bytes(suffix_in.at[b, others], suffix_recv.at[b])
        for h in range(b * GROUP, (b + 1) * GROUP):
            later_b = get_state(suffix_in, h).astype(BF16)
            grad_k = part_k[h] + of_key[h] * matmul(v_ref[0, :, columns(h)], later_b, 1, 1)
            grad_v = part_v[h] + of_key[h] * matmul(k_ref[0, :, columns(h)], later_b, 1, 0)
            gk_ref[0, :, columns(h)] = grad_k.astype(BF16)
            gv_ref[0, :, columns(h)] = grad_v.astype(BF16)

    other_core.wait()
    gg_ref[...] = gain_total + gain_dp_in[...]

    for b in range(BATCHES):
        wait_bytes(state.at[b, others, FULL], state_send.at[b])
        row_sent(row_out.at[b], row_send.at[b], True)
        wait_bytes(prefix.at[b, others], prefix_send.at[b])
        wait_bytes(back.at[b, others], back_send.at[b])
        row_sent(row_back_out.at[b], row_back_send.at[b], False)
        wait_bytes(suffix.at[b, others], suffix_send.at[b])
    wait_bytes(norm_in.at[pl.ds(0, TENSOR - 1)], norm_sems.at[0])
    wait_bytes(gain_y_in.at[pl.ds(0, RING - 1)], gain_y_sems.at[0])
    wait_bytes(gain_z_in.at[pl.ds(0, RING - 1)], gain_z_sems.at[0])


def store(*refs):
    sources, targets, sems = refs[:4], refs[4:8], refs[8]
    copies = [
        pltpu.make_async_copy(source, target, sems.at[i])
        for i, (source, target) in enumerate(zip(sources, targets))
    ]
    for copy in copies:
        copy.start()
    for copy in copies:
        copy.wait()


def shards(queries, keys, values, forget, gain, grad_out):
    block = jax.ShapeDtypeStruct(queries.shape, BF16)
    rows = pltpu.VMEM((BATCHES, RING, ROWS, E), F32)
    rows_more = pltpu.VMEM((BATCHES, RING, ROWS + 8, E), F32)
    total = pltpu.VMEM((BATCHES, ROWS + 8, E), F32)
    first = [rows_more, rows_more, total, rows_more, rows, rows]
    second = [rows, rows, total, rows_more, rows, rows]
    squares_f32 = pltpu.VMEM((HEADS, E, E), F32)
    squares_bf16 = pltpu.VMEM((HEADS, E, E), BF16)
    tile = pltpu.VMEM((8, E), F32)
    ring = pltpu.VMEM((RING, 8, E), F32)
    pair = pltpu.SemaphoreType.DMA((2,))
    each = pltpu.SemaphoreType.DMA((BATCHES,))
    each_row = pltpu.SemaphoreType.DMA((BATCHES, RING))
    scan_sems = [each, each, each_row, each_row, each, each]
    vmem = pl.BlockSpec(memory_space=pltpu.VMEM)
    hbm = pl.BlockSpec(memory_space=pltpu.HBM)
    tokens = pltpu.VMEM(queries.shape, BF16)
    shapes = (block, block, block, jax.ShapeDtypeStruct((HEADS, E), F32))
    grads = pl.pallas_call(
        kernel,
        out_shape=shapes,
        in_specs=[hbm] * 6,
        out_specs=(vmem,) * 4,
        scratch_shapes=[tokens, tokens, tokens, pltpu.VMEM(forget.shape, F32), tile, tokens]
        + first
        + second
        + [squares_f32, squares_bf16, squares_f32, squares_bf16, squares_bf16]
        + [squares_f32] * 5
        + [squares_bf16]
        + [tile, pltpu.VMEM((TENSOR, 8, E), F32)]
        + [tile, ring, tile, ring, tile, tile]
        + scan_sems * 2
        + [pair] * 4
        + [pltpu.SemaphoreType.DMA((6,))],
        compiler_params=pltpu.CompilerParams(
            collective_id=0, has_side_effects=True, vmem_limit_bytes=40 << 20
        ),
    )(
        *(
            pltpu.with_memory_space_constraint(x, pltpu.HBM)
            for x in (queries, keys, values, forget, gain.reshape(HEADS, E), grad_out)
        )
    )
    grad_q, grad_k, grad_v, grad_gain = pl.pallas_call(
        store,
        out_shape=shapes,
        in_specs=[vmem] * 4,
        out_specs=(hbm,) * 4,
        scratch_shapes=[pltpu.SemaphoreType.DMA((4,))],
        compiler_params=pltpu.CompilerParams(vmem_limit_bytes=4 << 20),
    )(*grads)
    return grad_q, grad_k, grad_v, grad_gain.reshape(-1)


def solution(mesh):
    in_specs = (
        P("dp", "ctx", "tensor"),
        P("dp", "ctx", "tensor"),
        P("dp", "ctx", "tensor"),
        P("dp", "tensor", "ctx"),
        P("tensor"),
        P("dp", "ctx", "tensor"),
    )
    out_specs = (
        P("dp", "ctx", "tensor"),
        P("dp", "ctx", "tensor"),
        P("dp", "ctx", "tensor"),
        P("tensor"),
    )
    return jax.shard_map(shards, mesh=mesh, in_specs=in_specs, out_specs=out_specs, check_vma=False)
```

```python
import functools

import jax
import jax.numpy as jnp
from jax import lax
from jax.experimental import pallas as pl
from jax.experimental.pallas import tpu as pltpu
from jax.sharding import PartitionSpec as P

E = 128
EPSILON = 1e-05
MESH = pl.DeviceIdType.MESH
F32 = jnp.float32
BF16 = jnp.bfloat16

HEADS = 8
RING = 8
FAR_FIRST = (4, 3, 5, 2, 6, 1, 7)
TENSOR = 4
BATCHES = 4
GROUP = HEADS // BATCHES
SPLIT = RING // GROUP
ROWS = E // SPLIT
PART = pl.ds(0, ROWS)
FULL = pl.ds(0, ROWS + 1)


def matmul(a, b, contract_a, contract_b):
    return lax.dot_general(
        a, b, (((contract_a,), (contract_b,)), ((), ())), preferred_element_type=F32
    )


def kernel(
    q_hbm, k_hbm, v_hbm, f_hbm, gain_hbm, g_hbm,
    gq_ref, gk_ref, gv_ref, gg_ref,
    q_ref, k_ref, v_ref, f_ref, gain_ref, g_ref,
    state, state_in, row_out, row_in, prefix, prefix_in,
    back, back_in, row_back_out, row_back_in, suffix, suffix_in,
    weight, weighted, attended, earlier_b, grad_att, part_k, part_v,
    grad_normed, of_query, of_key, query_scaled,
    norm_out, norm_in,
    gain_y_out, gain_y_in, gain_z_out, gain_z_in, gain_dp_out, gain_dp_in,
    state_send, state_recv, row_send, row_recv, prefix_send, prefix_recv,
    back_send, back_recv, row_back_send, row_back_recv, suffix_send, suffix_recv,
    norm_sems, gain_y_sems, gain_z_sems, gain_dp_sems, load_sems,
):
    dp, me, tn = lax.axis_index("dp"), lax.axis_index("ctx"), lax.axis_index("tensor")
    z, y = me // RING, lax.rem(me, RING)
    scale = E ** (-0.5)
    full_width = TENSOR * HEADS * E

    def tensor_peer(i):
        return lax.rem(tn + i, TENSOR)

    def y_peer(i):
        return z * RING + lax.rem(y + i, RING)

    def z_peer(i):
        return lax.rem(z + i, RING) * RING + y

    barrier = pltpu.get_barrier_semaphore()

    loads = [
        pltpu.make_async_copy(source, target, load_sems.at[i])
        for i, (source, target) in enumerate(
            (
                (f_hbm, f_ref), (k_hbm, k_ref), (v_hbm, v_ref),
                (q_hbm, q_ref), (g_hbm, g_ref), (gain_hbm, gain_ref),
            )
        )
    ]
    for load in loads:
        load.start()

    for i in range(1, RING):
        for peer in (y_peer(i), z_peer(i)):
            pl.semaphore_signal(barrier, inc=1, device_id=(dp, peer, tn), device_id_type=MESH)
    for i in range(1, TENSOR):
        pl.semaphore_signal(
            barrier, inc=1, device_id=(dp, me, tensor_peer(i)), device_id_type=MESH
        )
    pl.semaphore_signal(barrier, inc=1, device_id=(1 - dp, me, tn), device_id_type=MESH)
    greeted = 2 * (RING - 1) + TENSOR - 1 + 1

    def remote(src, dst, send_sem, recv_sem, device):
        return pltpu.make_async_remote_copy(
            src_ref=src, dst_ref=dst, send_sem=send_sem, recv_sem=recv_sem,
            device_id=device, device_id_type=MESH,
        )

    def wait_bytes(ref, sem):
        pltpu.make_async_copy(ref, ref, sem).wait()

    others = pl.ds(0, RING - 1)

    def exchange(src, dst, send_sem, recv_sem, rows):
        for i in FAR_FIRST:
            peer = lax.rem(y + i, RING)
            remote(
                src.at[peer, rows], dst.at[y, rows], send_sem, recv_sem,
                (dp, z * RING + peer, tn),
            ).start()
        dst[y, rows] = src[y, rows]

    def row_peers(later):
        for i in range(RING - 1, 0, -1):
            peer = z + i if later else z - i
            yield i, peer, (peer < RING) if later else (peer >= 0)

    def send_row(out, into, send_sems, recv_sems, later):
        for i, peer, exists in row_peers(later):

            @pl.when(exists)
            def _(i=i, peer=peer):
                remote(
                    out.at[FULL], into.at[z, FULL], send_sems.at[i], recv_sems.at[z],
                    (dp, peer * RING + y, tn),
                ).start()

    def row_sent(out, send_sems, later):
        for i, _, exists in row_peers(later):

            @pl.when(exists)
            def _(i=i):
                wait_bytes(out.at[FULL], send_sems.at[i])

    def row_arrived(into, recv_sems, later):
        for i, peer, exists in row_peers(not later):

            @pl.when(exists)
            def _(peer=peer):
                wait_bytes(into.at[peer, FULL], recv_sems.at[peer])

    def row_total(source, decays, out, reverse):
        total = jnp.zeros((ROWS, E), F32)
        decay = jnp.ones((1, E), F32)
        for at in range(RING - 1, -1, -1) if reverse else range(RING):
            passed = decays[at, ROWS : ROWS + 1]
            total = total * passed + source[at]
            decay = decay * passed
        out[0:ROWS] = total
        out[ROWS : ROWS + 1] = decay

    def run_scan(source, decays, rows, result, reverse):
        def of_row(i, total):
            at = RING - 1 - i if reverse else i
            return total * rows[at, ROWS : ROWS + 1] + rows[at, 0:ROWS]

        total = lax.fori_loop(
            0, RING - 1 - z if reverse else z, of_row, jnp.zeros((ROWS, E), F32)
        )
        for at in range(RING - 1, -1, -1) if reverse else range(RING):
            result[at] = total
            total = total * decays[at, ROWS : ROWS + 1] + source[at]

    loads[0].wait()
    lanes = lax.broadcasted_iota(jnp.int32, (HEADS, E), 1)
    cumulative = f_ref[0]
    for shift in (1, 2, 4, 8, 16, 32, 64):
        moved = pltpu.roll(cumulative, shift, 1)
        cumulative = cumulative + jnp.where(lanes >= shift, moved, 0.0)
    block_decay = cumulative[:, E - 1 :]
    passing = jnp.broadcast_to(jnp.exp(-block_decay), (HEADS, E))
    cumulative_t = cumulative.T
    query_decay = jnp.exp(-cumulative).T
    key_decay = jnp.exp(-(block_decay - cumulative)).T

    def columns(h):
        return slice(h * E, (h + 1) * E)

    def pieces(h):
        return h // GROUP, slice((h % GROUP) * SPLIT, (h % GROUP + 1) * SPLIT)

    def put_state(ref, h, value):
        batch, owners = pieces(h)
        ref[batch, owners, 0:ROWS] = value.reshape(SPLIT, ROWS, E)

    def get_state(ref, h):
        batch, owners = pieces(h)
        return ref[batch, owners].reshape(E, E)

    loads[1].wait()
    loads[2].wait()

    def make_state(h):
        key_scaled = (k_ref[0, :, columns(h)].astype(F32) * key_decay[:, h : h + 1]).astype(BF16)
        put_state(state, h, matmul(key_scaled, v_ref[0, :, columns(h)], 0, 0))
        batch, owners = pieces(h)
        state[batch, owners, ROWS : ROWS + 1] = jnp.broadcast_to(passing[h], (SPLIT, 1, E))

    for h in range(HEADS):
        make_state(h)
    pl.semaphore_wait(barrier, greeted)
    for b in range(BATCHES):
        exchange(state.at[b], state_in.at[b], state_send.at[b], state_recv.at[b], FULL)
    for load in loads[3:]:
        load.wait()

    below = lax.broadcasted_iota(jnp.int32, (E, E), 0) >= lax.broadcasted_iota(
        jnp.int32, (E, E), 1
    )

    def make_local(h):
        span = cumulative_t[:, h : h + 1] - cumulative[h : h + 1, :]
        now = jnp.where(below, jnp.exp(-jnp.where(below, span, 0.0)), 0.0)
        weight[h] = now
        scores = matmul(q_ref[0, :, columns(h)], k_ref[0, :, columns(h)], 1, 1)
        rounded = (scores * scale * now).astype(BF16)
        weighted[h] = rounded
        attended[h] = matmul(rounded, v_ref[0, :, columns(h)], 1, 0)
        grad_normed[h] = g_ref[0, :, columns(h)].astype(F32) * gain_ref[h : h + 1, :]
        of_query[h] = jnp.broadcast_to(scale * query_decay[:, h : h + 1], (E, E))
        of_key[h] = jnp.broadcast_to(scale * key_decay[:, h : h + 1], (E, E))
        scaled = q_ref[0, :, columns(h)].astype(F32) * query_decay[:, h : h + 1]
        query_scaled[h] = scaled.T.astype(BF16)

    for h in range(HEADS):
        make_local(h)
    for b in range(BATCHES):
        wait_bytes(state_in.at[b, others, FULL], state_recv.at[b])
        row_total(state_in.at[b, :, 0:ROWS], state_in.at[b], row_out.at[b], False)
        send_row(row_out.at[b], row_in.at[b], row_send.at[b], row_recv.at[b], True)
    for b in range(BATCHES):
        row_arrived(row_in.at[b], row_recv.at[b], True)
        run_scan(state_in.at[b, :, 0:ROWS], state_in.at[b], row_in.at[b], prefix.at[b], False)
        exchange(
            prefix.at[b], prefix_in.at[b], prefix_send.at[b], prefix_recv.at[b], PART
        )

    squares = jnp.zeros((E, E), F32)
    products = jnp.zeros((E, E), F32)
    for b in range(BATCHES):
        wait_bytes(prefix_in.at[b, others], prefix_recv.at[b])
        for h in range(b * GROUP, (b + 1) * GROUP):
            state_b = get_state(prefix_in, h).astype(BF16)
            earlier_b[h] = state_b
            carried = matmul(q_ref[0, :, columns(h)], state_b, 1, 0)
            now = attended[h] + of_query[h] * carried
            attended[h] = now
            squares = squares + now * now
            products = products + grad_normed[h] * now

    wide = lax.broadcasted_iota(jnp.int32, (E, E), 1)
    both = jnp.where(
        wide == 0,
        jnp.sum(squares, axis=1, keepdims=True),
        jnp.sum(products, axis=1, keepdims=True),
    ).T[0:8]
    norm_out[...] = both

    def send_norm(i, carry):
        remote(
            norm_out, norm_in.at[tn], norm_sems.at[0], norm_sems.at[1], (dp, me, tensor_peer(i))
        ).start()
        return carry

    lax.fori_loop(1, TENSOR, send_norm, 0)
    norm_in[tn] = both
    wait_bytes(norm_in.at[pl.ds(0, TENSOR - 1)], norm_sems.at[1])
    sums = (norm_in[0] + norm_in[1]) + (norm_in[2] + norm_in[3])
    inverse_rms = lax.rsqrt(sums[0:1] / full_width + EPSILON)
    projected = sums[1:2] * inverse_rms / full_width
    of_grad = jnp.broadcast_to(inverse_rms, (E, E)).T
    of_attended = jnp.broadcast_to(inverse_rms * inverse_rms * projected, (E, E)).T

    def make_back(b):
        for h in range(b * GROUP, (b + 1) * GROUP):
            grad_now = (of_grad * grad_normed[h] - of_attended * attended[h]).astype(BF16)
            grad_att[h] = grad_now
            put_state(back, h, matmul(query_scaled[h], grad_now, 1, 0))
        exchange(back.at[b], back_in.at[b], back_send.at[b], back_recv.at[b], PART)

    def sum_ring(out, into, sems, peer_of, mine):
        def go(i, carry):
            remote(out, into.at[mine], sems.at[0], sems.at[1], (dp, peer_of(i), tn)).start()
            return carry

        lax.fori_loop(1, RING, go, 0)
        into[mine] = out[...]

    def ring_total(into, sems):
        wait_bytes(into.at[pl.ds(0, RING - 1)], sems.at[1])
        total = into[0]
        for i in range(1, RING):
            total = total + into[i]
        return total

    for b in range(BATCHES):
        make_back(b)
    for h in range(HEADS):
        normed = attended[h] * of_grad
        gain_y_out[h] = jnp.sum(g_ref[0, :, columns(h)].astype(F32) * normed, axis=0)
    sum_ring(gain_y_out, gain_y_in, gain_y_sems, y_peer, y)

    def make_parts(h):
        grad_now = grad_att[h]
        scores = matmul(grad_now, v_ref[0, :, columns(h)], 1, 1)
        grad_weighted = (scores * scale * weight[h]).astype(BF16)
        grad_q = matmul(grad_weighted, k_ref[0, :, columns(h)], 1, 0) + of_query[h] * matmul(
            grad_now, earlier_b[h], 1, 1
        )
        gq_ref[0, :, columns(h)] = grad_q.astype(BF16)
        part_k[h] = matmul(grad_weighted, q_ref[0, :, columns(h)], 0, 0)
        part_v[h] = matmul(weighted[h], grad_now, 0, 0)

    for h in range(HEADS):
        make_parts(h)
    for b in range(BATCHES):
        wait_bytes(back_in.at[b, others], back_recv.at[b])
        row_total(back_in.at[b], state_in.at[b], row_back_out.at[b], True)
        send_row(
            row_back_out.at[b], row_back_in.at[b], row_back_send.at[b], row_back_recv.at[b], False
        )
    gain_z_out[...] = ring_total(gain_y_in, gain_y_sems)
    sum_ring(gain_z_out, gain_z_in, gain_z_sems, z_peer, z)
    for b in range(BATCHES):
        row_arrived(row_back_in.at[b], row_back_recv.at[b], False)
        run_scan(back_in.at[b], state_in.at[b], row_back_in.at[b], suffix.at[b], True)
        exchange(
            suffix.at[b], suffix_in.at[b], suffix_send.at[b], suffix_recv.at[b], PART
        )
    gain_total = ring_total(gain_z_in, gain_z_sems)
    gain_dp_out[...] = gain_total
    other_core = remote(
        gain_dp_out, gain_dp_in, gain_dp_sems.at[0], gain_dp_sems.at[1], (1 - dp, me, tn)
    )
    other_core.start()
    for b in range(BATCHES):
        wait_bytes(state.at[b, others, FULL], state_send.at[b])
        row_sent(row_out.at[b], row_send.at[b], True)
        wait_bytes(prefix.at[b, others], prefix_send.at[b])
        wait_bytes(back.at[b, others], back_send.at[b])
        row_sent(row_back_out.at[b], row_back_send.at[b], False)
    wait_bytes(norm_in.at[pl.ds(0, TENSOR - 1)], norm_sems.at[0])
    wait_bytes(gain_y_in.at[pl.ds(0, RING - 1)], gain_y_sems.at[0])
    wait_bytes(gain_z_in.at[pl.ds(0, RING - 1)], gain_z_sems.at[0])
    for b in range(BATCHES):
        wait_bytes(suffix_in.at[b, others], suffix_recv.at[b])
        for h in range(b * GROUP, (b + 1) * GROUP):
            later_b = get_state(suffix_in, h).astype(BF16)
            grad_k = part_k[h] + of_key[h] * matmul(v_ref[0, :, columns(h)], later_b, 1, 1)
            grad_v = part_v[h] + of_key[h] * matmul(k_ref[0, :, columns(h)], later_b, 1, 0)
            gk_ref[0, :, columns(h)] = grad_k.astype(BF16)
            gv_ref[0, :, columns(h)] = grad_v.astype(BF16)

    other_core.wait()
    gg_ref[...] = gain_total + gain_dp_in[...]

    for b in range(BATCHES):
        wait_bytes(suffix.at[b, others], suffix_send.at[b])


def store(*refs):
    sources, targets, sems = refs[:4], refs[4:8], refs[8]
    copies = [
        pltpu.make_async_copy(source, target, sems.at[i])
        for i, (source, target) in enumerate(zip(sources, targets))
    ]
    for copy in copies:
        copy.start()
    for copy in copies:
        copy.wait()


def shards(queries, keys, values, forget, gain, grad_out):
    block = jax.ShapeDtypeStruct(queries.shape, BF16)
    rows = pltpu.VMEM((BATCHES, RING, ROWS, E), F32)
    rows_more = pltpu.VMEM((BATCHES, RING, ROWS + 8, E), F32)
    total = pltpu.VMEM((BATCHES, ROWS + 8, E), F32)
    first = [rows_more, rows_more, total, rows_more, rows, rows]
    second = [rows, rows, total, rows_more, rows, rows]
    squares_f32 = pltpu.VMEM((HEADS, E, E), F32)
    squares_bf16 = pltpu.VMEM((HEADS, E, E), BF16)
    tile = pltpu.VMEM((8, E), F32)
    ring = pltpu.VMEM((RING, 8, E), F32)
    pair = pltpu.SemaphoreType.DMA((2,))
    each = pltpu.SemaphoreType.DMA((BATCHES,))
    each_row = pltpu.SemaphoreType.DMA((BATCHES, RING))
    scan_sems = [each, each, each_row, each_row, each, each]
    vmem = pl.BlockSpec(memory_space=pltpu.VMEM)
    hbm = pl.BlockSpec(memory_space=pltpu.HBM)
    tokens = pltpu.VMEM(queries.shape, BF16)
    shapes = (block, block, block, jax.ShapeDtypeStruct((HEADS, E), F32))
    grads = pl.pallas_call(
        kernel,
        out_shape=shapes,
        in_specs=[hbm] * 6,
        out_specs=(vmem,) * 4,
        scratch_shapes=[tokens, tokens, tokens, pltpu.VMEM(forget.shape, F32), tile, tokens]
        + first
        + second
        + [squares_f32, squares_bf16, squares_f32, squares_bf16, squares_bf16]
        + [squares_f32] * 5
        + [squares_bf16]
        + [tile, pltpu.VMEM((TENSOR, 8, E), F32)]
        + [tile, ring, tile, ring, tile, tile]
        + scan_sems * 2
        + [pair] * 4
        + [pltpu.SemaphoreType.DMA((6,))],
        compiler_params=pltpu.CompilerParams(
            collective_id=0, has_side_effects=True, vmem_limit_bytes=40 << 20
        ),
    )(
        *(
            pltpu.with_memory_space_constraint(x, pltpu.HBM)
            for x in (queries, keys, values, forget, gain.reshape(HEADS, E), grad_out)
        )
    )
    grad_q, grad_k, grad_v, grad_gain = pl.pallas_call(
        store,
        out_shape=shapes,
        in_specs=[vmem] * 4,
        out_specs=(hbm,) * 4,
        scratch_shapes=[pltpu.SemaphoreType.DMA((4,))],
        compiler_params=pltpu.CompilerParams(vmem_limit_bytes=4 << 20),
    )(*grads)
    return grad_q, grad_k, grad_v, grad_gain.reshape(-1)


def solution(mesh):
    in_specs = (
        P("dp", "ctx", "tensor"),
        P("dp", "ctx", "tensor"),
        P("dp", "ctx", "tensor"),
        P("dp", "tensor", "ctx"),
        P("tensor"),
        P("dp", "ctx", "tensor"),
    )
    out_specs = (
        P("dp", "ctx", "tensor"),
        P("dp", "ctx", "tensor"),
        P("dp", "ctx", "tensor"),
        P("tensor"),
    )
    return jax.shard_map(shards, mesh=mesh, in_specs=in_specs, out_specs=out_specs, check_vma=False)
```
